512 devices in a mesh: gx: 16 (over z, core), gy: 4 (over y_hi), gz: 8 (over y_lo, x).
Axes of the slice: x: 4, y: 8 (y_hi: 4, y_lo: 2; y = y_hi * 2 + y_lo), z: 8, core: 2. Of those that a mesh axis runs over, the one named last changes fastest.
Arguments:
- features: bfloat16 [16, 4, 8, 128, 128], P('gx', 'gy', 'gz'), may hold values from -6 to 6
- positions: float32 [16, 4, 8, 3, 128], P('gx', 'gy', 'gz'), may hold values from 0 to 11
- w_up: bfloat16 [128, 128], replicated, may hold values from -0.5 to 0.5
- w_basis: float32 [8, 64], replicated, may hold values from -2 to 2
- w_hidden: bfloat16 [64, 64], replicated, may hold values from -0.75 to 0.75
- w_radial: bfloat16 [64, 384], replicated, may hold values from -0.75 to 0.75
- w_mix: bfloat16 [384, 128], replicated, may hold values from -0.3125 to 0.3125
- w_read: float32 [128, 16], replicated, may hold values from -0.5 to 0.5
- w_out: float32 [16], replicated, may hold values from -1.5 to 1.5
- send_lists: int32 [16, 4, 8, 3, 3, 3, 64], P('gx', 'gy', 'gz'), may hold values from 0 to 127, as said below
- tile_senders: int32 [16, 4, 8, 64, 128], P('gx', 'gy', 'gz'), may hold values from 0 to 1807, as said below
- tile_slots: int32 [16, 4, 8, 64, 128], P('gx', 'gy', 'gz'), may hold values from 0 to 8, as said below
- tile_bases: int32 [16, 4, 8, 64], P('gx', 'gy', 'gz'), may hold values from 0 to 120
- tile_live: int32 [16, 4, 8], P('gx', 'gy', 'gz'), may hold values from 16 to 64, as said below
Outputs:
- forces: float32 [16, 4, 8, 3, 128], P('gx', 'gy', 'gz')
- atom_energy: float32 [16, 4, 8, 128], P('gx', 'gy', 'gz')
The draws below stay inside these ranges and needn't reach their ends.
Inputs may be any that keep to these rules, and one draw needn't show every extreme that they name: `send_lists`: for direction (dx, dy, dz), entry [.., 1 + dx, 1 + dy, 1 + dz, s] names an atom of the device; with k nonzero components the first 64 * 2 / 2**k entries (k of 1 to 3) name distinct atoms, those lying in the half of the cube toward each nonzero component, and later entries name other atoms. The list with dx = dy = dz = 0 is never read. `tile_senders`: below 128: an atom of the device. Else 128 + b * 64 + s: entry s of the atoms arriving from direction b; b = 13 never occurs, and s < 64 * 2 / 2**k for k nonzero components of the direction. `tile_slots`: the value 8 marks an unused edge. `tile_live`: A quarter of the devices have 64 live tiles, the others between 16 and 21.
All inputs are finite; a program needn't handle non-finite values.
Results may differ from the reference program's by a relative error of at most 0.022.
Values may be sent and summed in bfloat16 or wider, within the bound.
A program may use at most 64 MiB of HBM per device.

```python
import jax
import jax.numpy as jnp
from jax import lax

C = 128
RH = 64
RO = 16
NB = 8
RT = 8
EDGE = 128
ATOMS = 128
TILES = 64
SLOTS = 64
BX = 16
BY = 4
BZ = 8


def cell_layout(key):
    devices_all = BX * BY * BZ
    subkeys = jax.random.split(jax.random.fold_in(key, 101), devices_all)
    ordering = jax.vmap(lambda single: jax.random.permutation(single, ATOMS))(subkeys).astype(jnp.int32)
    cell_ids = ordering // (ATOMS // 8)
    cell_bits = jnp.stack([cell_ids // 4, cell_ids // 2 % 2, cell_ids % 2], axis=1)
    return (ordering, cell_bits)


def direction_table():
    step_ids = jnp.arange(27, dtype=jnp.int32)
    return jnp.stack([step_ids // 9 - 1, step_ids // 3 % 3 - 1, step_ids % 3 - 1], axis=1)


def tile_plan(key):
    ordering, cell_bits = cell_layout(key)
    devices_all = BX * BY * BZ
    planner = jax.random.fold_in(key, 202)
    subkeys = jax.random.split(planner, 8)
    ranking = jax.random.permutation(subkeys[0], devices_all)
    light_len = TILES // 4 + jax.random.randint(subkeys[1], (devices_all,), 0, TILES // 3 - TILES // 4 + 1)
    live_count = jnp.where(ranking < devices_all // 4, TILES, light_len)
    live_count = jnp.where(ranking == devices_all - 1, TILES // 4, live_count).astype(jnp.int32)
    tile_index = jnp.arange(TILES, dtype=jnp.int32)[None, :]
    spaced = tile_index * (ATOMS - RT) // jnp.maximum(live_count[:, None] - 1, 1)
    loose = jax.random.randint(subkeys[2], (devices_all, TILES), 0, ATOMS - RT + 1)
    bases = jnp.where(tile_index < live_count[:, None], spaced, loose).astype(jnp.int32)
    slot_ids = jax.random.randint(subkeys[3], (devices_all, TILES, EDGE), 0, RT)
    unused = jax.random.randint(subkeys[4], (devices_all, TILES, EDGE), 0, 8) == 0
    slot_ids = jnp.where(unused, RT, slot_ids)
    slot_ids = slot_ids.at[:, 0, 1].set(RT).astype(jnp.int32)
    receiver = bases[:, :, None] + jnp.minimum(slot_ids, RT - 1)
    receiver_bits = jax.vmap(lambda bits_one, rows_one: bits_one[:, rows_one])(cell_bits, receiver)
    moves = jax.random.randint(subkeys[5], (devices_all, 3, TILES, EDGE), -1, 2)
    target = receiver_bits + moves
    offset = jnp.floor_divide(target, 2)
    target_cell = target - 2 * offset
    cell_index = target_cell[:, 0] * 4 + target_cell[:, 1] * 2 + target_cell[:, 2]
    member = jax.random.randint(subkeys[6], (devices_all, TILES, EDGE), 0, ATOMS // 8)
    inverse = jnp.argsort(ordering, axis=-1, stable=True).astype(jnp.int32)
    own_atom = jax.vmap(lambda inverse_one, wanted: inverse_one[wanted])(inverse, cell_index * (ATOMS // 8) + member)
    block_id = (offset[:, 0] + 1) * 9 + (offset[:, 1] + 1) * 3 + offset[:, 2] + 1
    nonzero = jnp.sum((offset != 0).astype(jnp.int32), axis=1)
    count_valid = jnp.where(nonzero <= 1, SLOTS, jnp.where(nonzero == 2, SLOTS // 2, SLOTS // 4))
    picked = jax.random.randint(subkeys[7], (devices_all, TILES, EDGE), 0, 1 << 20) % count_valid
    remote = ATOMS + block_id * SLOTS + picked
    senders = jnp.where(nonzero == 0, own_atom, remote)
    senders = senders.at[:, 0, 0].set(ATOMS + 26 * SLOTS + SLOTS // 4 - 1).astype(jnp.int32)
    return (senders, slot_ids, bases, live_count)


def draw_positions(key, part):
    ordering, cell_bits = cell_layout(key)
    key = jax.random.fold_in(key, 1)
    pick_key, place_key = jax.random.split(key)
    chooser = jax.random.uniform(pick_key, cell_bits.shape, jnp.float32)
    spread = jax.random.uniform(place_key, cell_bits.shape, jnp.float32)
    depth = jnp.where(chooser < 0.4, 0.8 * spread, jnp.where(chooser < 0.8, 4.0 + spread, 5.5 * spread))
    coords = jnp.where(cell_bits == 1, 11.0 - depth, depth)
    return coords.reshape(BX, BY, BZ, 3, ATOMS)


def draw_send_lists(key, part):
    ordering, cell_bits = cell_layout(key)
    key = jax.random.fold_in(key, 2)
    devices_all = BX * BY * BZ
    offsets = direction_table()[None, :, :, None]
    bits_all = cell_bits[:, None, :, :]
    matched = jnp.all((offsets == 0) | (offsets == 1) & (bits_all == 1) | (offsets == -1) & (bits_all == 0), axis=2)
    subkeys = jax.random.split(key, devices_all * 27)
    ranking = jax.vmap(lambda single: jax.random.permutation(single, ATOMS))(subkeys).reshape(devices_all, 27, ATOMS)
    scores = jnp.where(matched, 0, ATOMS) + ranking
    chosen = jnp.argsort(scores, axis=-1, stable=True)[:, :, :SLOTS].astype(jnp.int32)
    return chosen.reshape(BX, BY, BZ, 3, 3, 3, SLOTS)


def draw_tile_senders(key, part):
    senders, slot_ids, bases, live_count = tile_plan(key)
    return senders.reshape(BX, BY, BZ, TILES, EDGE)


def draw_tile_slots(key, part):
    senders, slot_ids, bases, live_count = tile_plan(key)
    return slot_ids.reshape(BX, BY, BZ, TILES, EDGE)


def draw_tile_bases(key, part):
    senders, slot_ids, bases, live_count = tile_plan(key)
    return bases.reshape(BX, BY, BZ, TILES)


def draw_tile_live(key, part):
    senders, slot_ids, bases, live_count = tile_plan(key)
    return live_count.reshape(BX, BY, BZ)


def block_levels(key, shape, cuts, low, largest):
    gain = 1.0
    for dim, shards_of in cuts:
        steps = jax.random.uniform(jax.random.fold_in(jax.random.fold_in(key, 6), dim), (shards_of,), jnp.float32, low / len(cuts), largest / len(cuts))
        gain = gain * jnp.repeat(jnp.exp(steps), shape[dim] // shards_of).reshape((-1,) + (1,) * (len(shape) - 1 - dim))
    return gain


def scatter_about(own_key, shape, scale, bound, cuts=(), held_as=jnp.bfloat16):
    factor_of = block_levels(own_key, shape, cuts, -0.22, 0.18) if cuts else 1.0
    drawn = jax.random.normal(own_key, shape, jnp.float32) * scale * factor_of
    return jnp.minimum(jnp.maximum(drawn, -bound), bound).astype(held_as)


def setup_inputs(seed: int = 0) -> dict:
    arg_keys = jax.random.split(jax.random.key(seed), 15)
    return {
        "features": scatter_about(arg_keys[0], (BX, BY, BZ, ATOMS, C), 1.0, 6.0, ((0, 16), (1, 4), (2, 8))),
        "positions": draw_positions(jax.random.fold_in(arg_keys[14], 71), 0),
        "w_up": scatter_about(arg_keys[2], (C, C), C ** -0.5, 0.5),
        "w_basis": scatter_about(arg_keys[3], (NB, RH), NB ** -0.5, 2.0, (), jnp.float32),
        "w_hidden": scatter_about(arg_keys[4], (RH, RH), RH ** -0.5, 0.75),
        "w_radial": scatter_about(arg_keys[5], (RH, 3 * C), RH ** -0.5, 0.75),
        "w_mix": scatter_about(arg_keys[6], (3 * C, C), (3 * C) ** -0.5, 0.3125),
        "w_read": scatter_about(arg_keys[7], (C, RO), C ** -0.5, 0.5, (), jnp.float32),
        "w_out": scatter_about(arg_keys[8], (RO,), RO ** -0.5, 1.5, (), jnp.float32),
        "send_lists": draw_send_lists(jax.random.fold_in(arg_keys[14], 71), 0),
        "tile_senders": draw_tile_senders(jax.random.fold_in(arg_keys[14], 71), 0),
        "tile_slots": draw_tile_slots(jax.random.fold_in(arg_keys[14], 71), 0),
        "tile_bases": draw_tile_bases(jax.random.fold_in(arg_keys[14], 71), 0),
        "tile_live": draw_tile_live(jax.random.fold_in(arg_keys[14], 71), 0),
    }


inv_cutoff = 0.2
domain_side = 11.0
sums_scale = 0.5

def harmonics(scaled):
    xcoord = scaled[0]
    ycoord = scaled[1]
    zcoord = scaled[2]
    root_three = 3.0 ** 0.5
    root_five = 5.0 ** 0.5
    root_fifteen = 15.0 ** 0.5
    pieces = [jnp.ones_like(xcoord), root_three * xcoord, root_three * ycoord, root_three * zcoord, root_fifteen * xcoord * ycoord, root_fifteen * ycoord * zcoord, 0.5 * root_five * (2.0 * zcoord * zcoord - xcoord * xcoord - ycoord * ycoord), root_fifteen * xcoord * zcoord, 0.5 * root_fifteen * (xcoord * xcoord - ycoord * ycoord)]
    return jnp.stack(pieces, axis=0)

def tile_sums(separation, sender_rows, slot_ids, w_basis, w_hidden, w_radial):
    edge_count, channels = sender_rows.shape
    scaled = separation * inv_cutoff
    radius_sq = lax.optimization_barrier(jnp.sum(scaled * scaled, axis=0))
    envelope = jnp.maximum(1.0 - radius_sq * radius_sq, 0.0) ** 2
    decays = (jnp.arange(w_basis.shape[0], dtype=jnp.float32) + 1.0) * 0.5
    radial_basis = jnp.exp(-decays[:, None] * radius_sq[None, :]) * envelope[None, :]
    hidden_one = jax.nn.silu(jnp.dot(radial_basis.T, w_basis, precision=lax.Precision.HIGHEST)).astype(jnp.bfloat16)
    hidden_two = jax.nn.silu(jnp.dot(hidden_one, w_hidden, preferred_element_type=jnp.float32)).astype(jnp.bfloat16)
    radial = jnp.dot(hidden_two, w_radial, preferred_element_type=jnp.float32).reshape(edge_count, 3, channels)
    widened = jnp.concatenate([radial[:, 0:1], jnp.broadcast_to(radial[:, 1:2], (edge_count, 3, channels)), jnp.broadcast_to(radial[:, 2:3], (edge_count, 5, channels))], axis=1)
    angular = harmonics(scaled).T
    message = (widened * angular[:, :, None] * sender_rows.astype(jnp.float32)[:, None, :]).astype(jnp.bfloat16)
    onehot = (slot_ids[None, :] == jnp.arange(RT, dtype=jnp.int32)[:, None]).astype(jnp.bfloat16)
    product = jnp.dot(onehot, message.reshape(edge_count, 9 * channels), preferred_element_type=jnp.float32)
    return product.reshape(RT, 9, channels)

def atom_energy_of(sums_in, own_rows, w_mix, w_read, w_out):
    scaled_sums = sums_in * sums_scale
    invariants = jnp.concatenate([scaled_sums[:, 0], lax.optimization_barrier(jnp.sum(scaled_sums[:, 1:4] ** 2, axis=1)), lax.optimization_barrier(jnp.sum(scaled_sums[:, 4:9] ** 2, axis=1))], axis=1).astype(jnp.bfloat16)
    updated = own_rows.astype(jnp.float32) + jnp.dot(invariants, w_mix, preferred_element_type=jnp.float32)
    readout = jax.nn.silu(jnp.dot(updated, w_read, precision=lax.Precision.HIGHEST))
    return jnp.dot(readout, w_out, precision=lax.Precision.HIGHEST)

def image_shift():
    offsets = jnp.arange(3, dtype=jnp.float32) - 1.0
    grids = jnp.meshgrid(offsets, offsets, offsets, indexing='ij')
    return jnp.stack(grids, axis=-1) * domain_side

def add_block(totals, tile_part, base_row):
    zero_index = base_row * 0
    current = lax.dynamic_slice(totals, (base_row, zero_index, zero_index), tile_part.shape)
    return lax.dynamic_update_slice(totals, current + tile_part, (base_row, zero_index, zero_index))

def reference(features, positions, w_up, w_basis, w_hidden, w_radial, w_mix, w_read, w_out, send_lists, tile_senders, tile_slots, tile_bases, tile_live):
    channels = features.shape[-1]
    projected = jnp.dot(features.reshape(-1, channels), w_up, preferred_element_type=jnp.float32)
    projected = projected.astype(jnp.bfloat16).reshape(BX, BY, BZ, ATOMS, channels)
    shifts = image_shift().reshape(27, 3)
    step_ids = jnp.arange(27, dtype=jnp.int32)
    step_one = step_ids // 9
    step_two = step_ids // 3 % 3
    step_three = step_ids % 3

    def device_energy(device_flat, coords):
        coord_one = device_flat // (BY * BZ)
        coord_two = device_flat // BZ % BY
        coord_three = device_flat % BZ
        near_one = (coord_one + step_one - 1) % BX
        near_two = (coord_two + step_two - 1) % BY
        near_three = (coord_three + step_three - 1) % BZ
        named_atoms = send_lists[near_one, near_two, near_three, 2 - step_one, 2 - step_two, 2 - step_three]
        in_rows = projected[near_one[:, None], near_two[:, None], near_three[:, None], named_atoms]
        in_rows = in_rows.reshape(27 * SLOTS, channels)
        in_coords = coords[near_one[:, None], near_two[:, None], near_three[:, None], :, named_atoms]
        in_coords = jnp.moveaxis(in_coords + shifts[:, None, :], 2, 0).reshape(3, 27 * SLOTS)
        own_coords = coords[coord_one, coord_two, coord_three]
        table_rows = jnp.concatenate([projected[coord_one, coord_two, coord_three], in_rows], axis=0)
        table_coords = jnp.concatenate([own_coords, in_coords], axis=1)
        senders = tile_senders[coord_one, coord_two, coord_three]
        slot_table = tile_slots[coord_one, coord_two, coord_three]
        base_table = tile_bases[coord_one, coord_two, coord_three]
        live_count = tile_live[coord_one, coord_two, coord_three]

        def step_tile(totals, tile_index):
            sender = senders[tile_index]
            slot_ids = slot_table[tile_index]
            base_row = base_table[tile_index]
            receiver = base_row + jnp.minimum(slot_ids, RT - 1)
            separation = table_coords[:, sender] - own_coords[:, receiver]
            tile_part = lax.cond(tile_index < live_count, lambda: tile_sums(separation, table_rows[sender], slot_ids, w_basis, w_hidden, w_radial), lambda: jnp.zeros((RT, 9, channels), totals.dtype))
            return (add_block(totals, tile_part, base_row), None)
        totals, _ = lax.scan(step_tile, jnp.zeros((ATOMS, 9, channels), jnp.float32), jnp.arange(TILES, dtype=jnp.int32))
        return atom_energy_of(totals, features[coord_one, coord_two, coord_three], w_mix, w_read, w_out)

    def total_energy(coords):
        per_device = lax.map(jax.checkpoint(lambda device_flat: device_energy(device_flat, coords)), jnp.arange(BX * BY * BZ, dtype=jnp.int32))
        return (jnp.sum(per_device), per_device)
    total, pullback, per_device = jax.vjp(total_energy, positions, has_aux=True)
    gradient, = pullback(jnp.ones_like(total))
    return (-gradient, per_device.reshape(BX, BY, BZ, ATOMS))
```

```python
import functools

import jax
import jax.numpy as jnp
from jax import lax
from jax.experimental import pallas as pl
from jax.experimental.pallas import tpu as pltpu
from jax.sharding import PartitionSpec as P

MESH = pl.DeviceIdType.MESH
F32 = jnp.float32
BF16 = jnp.bfloat16
I32 = jnp.int32

ATOMS = 128
C = 128
SLOTS = 64
TILES = 64
EDGE = 128
RT = 8
RH = 64
NB = 8
RO = 16
JR = TILES * RT
PE = 2 * EDGE
RP = 2 * RT
PER_STEP = 2
STEPS = TILES // 2 // PER_STEP
ES = PE * PER_STEP
TS = 2 * PER_STEP

SIDE = 11.0
INV_CUT = 0.2
R3 = 3.0**0.5
R5 = 5.0**0.5
R15 = 15.0**0.5
DEGREE = (0, 1, 1, 1, 2, 2, 2, 2, 2)
SPANS = ((0, 1), (1, 4), (4, 9))

DIRS = tuple((b // 9 - 1, b // 3 % 3 - 1, b % 3 - 1) for b in range(27))
NONZERO = tuple(sum(v != 0 for v in d) for d in DIRS)
COUNT = tuple(SLOTS * 2 // 2 ** max(k, 1) for k in NONZERO)
OTHERS = tuple(b for b in range(27) if b != 13)


def groups_of():
    groups = []
    for k in (1, 2, 3):
        here = [b for b in OTHERS if NONZERO[b] == k and b < 13]
        per = ATOMS // (SLOTS * 2 // 2**k) // 2
        for first in range(0, len(here), per):
            some = here[first : first + per]
            groups.append(tuple(some) + tuple(26 - b for b in some))
    return tuple(groups)


GROUPS = groups_of()
NG = len(GROUPS)
BLOCKS = NG + 1
GROUP = {b: g for g, some in enumerate(GROUPS) for b in some}
AT = {b: k * COUNT[b] for some in GROUPS for k, b in enumerate(some)}


def dot(a, b, ca, cb, precision=None):
    return lax.dot_general(
        a, b, (((ca,), (cb,)), ((), ())), preferred_element_type=F32, precision=precision
    )


def iota(shape, dim):
    return lax.broadcasted_iota(I32, shape, dim)


def hot(condition):
    return jnp.where(condition, 1.0, 0.0).astype(BF16)


def sigmoid(x):
    return 0.5 + 0.5 * jnp.tanh(0.5 * x)


def split(x):
    hi = x.astype(BF16)
    return hi, (x - hi.astype(F32)).astype(BF16)


def lanes(row, index):
    return jnp.take_along_axis(jnp.broadcast_to(row, index.shape), index, axis=1)


def kernel(
    sizes,
    feat_hbm,
    pos_hbm,
    wup_hbm,
    wbasis_hbm,
    whid_hbm,
    wrad_hbm,
    wmix_hbm,
    wread_hbm,
    wout_hbm,
    lists_hbm,
    send_hbm,
    slot_hbm,
    base_hbm,
    live_hbm,
    force_ref,
    energy_ref,
    feat_ref,
    pos_ref,
    wup_ref,
    wbasis_ref,
    whid_ref,
    wrad_ref,
    wmix_ref,
    wread_ref,
    wout_ref,
    lists_ref,
    send_ref,
    slot_ref,
    base_ref,
    live_ref,
    stage_sem,
    out_rows,
    out_xyz,
    table_b,
    in_xyz,
    table_t,
    table_c,
    chosen_ref,
    rows_ref,
    g_ref,
    a_ref,
    d1_ref,
    d2_ref,
    p_ref,
    s_ref,
    u_ref,
    rad_ref,
    slots_ref,
    low_ref,
    high_ref,
    target_ref,
    dharm_ref,
    drad_ref,
    gsep_ref,
    acc_ref,
    racc_ref,
    out_grad,
    in_grad,
    wbt_ref,
    wht_ref,
    wrt_ref,
    wb3_ref,
    row_send,
    row_recv,
    xyz_send,
    xyz_recv,
    grad_send,
    grad_recv,
):
    here = tuple(lax.axis_index(name) for name in ("gx", "gy", "gz"))

    def device(b):
        return tuple(lax.rem(c + (d + n), n) for c, d, n in zip(here, DIRS[b], sizes))

    barrier = pltpu.get_barrier_semaphore()
    for b in OTHERS:
        pl.semaphore_signal(barrier, inc=1, device_id=device(b), device_id_type=MESH)

    staged = {}
    moves = (
        ("feat", feat_hbm, feat_ref),
        ("wup", wup_hbm, wup_ref),
        ("lists", lists_hbm, lists_ref),
        ("pos", pos_hbm, pos_ref),
        ("base", base_hbm, base_ref),
        ("live", live_hbm, live_ref),
        ("slot", slot_hbm, slot_ref),
        ("send", send_hbm, send_ref),
        ("wbasis", wbasis_hbm, wbasis_ref),
        ("whid", whid_hbm, whid_ref),
        ("wrad", wrad_hbm, wrad_ref),
        ("wmix", wmix_hbm, wmix_ref),
        ("wread", wread_hbm, wread_ref),
        ("wout", wout_hbm, wout_ref),
    )
    for k, (name, source, target) in enumerate(moves):
        staged[name] = pltpu.make_async_copy(source, target, stage_sem.at[k])
        staged[name].start()
    early = ("feat", "wup", "lists", "pos")
    for name in early:
        staged[name].wait()

    projected = dot(feat_ref[...], wup_ref[...], 1, 0).astype(BF16)
    table_b[0:ATOMS, :] = projected
    own = jnp.concatenate([pos_ref[d] for d in range(3)], axis=0)
    lane = iota((1, 128), 1)
    for g, some in enumerate(GROUPS):
        order = sorted(some, key=lambda b: AT[26 - b])
        named = jnp.concatenate([lists_ref[b][:, 0 : COUNT[b]] for b in order], axis=1)
        chosen = hot(iota((ATOMS, 128), 0) == named)
        chosen_ref[g] = chosen
        out_rows[128 * g : 128 * g + 128, :] = dot(chosen, projected, 0, 0).astype(BF16)
        for d in range(3):
            shift = jnp.zeros((1, 128), F32)
            for b in some:
                if DIRS[b][d]:
                    inside = (lane >= AT[26 - b]) & (lane < AT[26 - b] + COUNT[b])
                    shift = jnp.where(inside, -SIDE * DIRS[b][d], shift)
            moved = lanes(own[d : d + 1, :], jnp.broadcast_to(named, (8, 128)))[0:1, :]
            out_xyz[g, d : d + 1, :] = moved + shift

    pl.semaphore_wait(barrier, 26)

    row_copies, xyz_copies = [], []
    for b in OTHERS:
        n, g, spot = COUNT[b], GROUP[b], AT[26 - b]
        row_copies.append(
            pltpu.make_async_remote_copy(
                src_ref=out_rows.at[pl.ds(128 * g + spot, n), :],
                dst_ref=table_b.at[pl.ds(128 * (g + 1) + spot, n), :],
                send_sem=row_send.at[b],
                recv_sem=row_recv.at[26 - b],
                device_id=device(b),
                device_id_type=MESH,
            )
        )
        xyz_copies.append(
            pltpu.make_async_remote_copy(
                src_ref=out_xyz.at[g],
                dst_ref=in_xyz.at[26 - b],
                send_sem=xyz_send.at[b],
                recv_sem=xyz_recv.at[26 - b],
                device_id=device(b),
                device_id_type=MESH,
            )
        )
    for one, two in zip(row_copies, xyz_copies):
        two.start()
        one.start()

    for name in staged:
        if name not in early:
            staged[name].wait()

    eye = hot(iota((128, 128), 0) == iota((128, 128), 1))
    eye64 = eye[0:64, 0:64]
    wb_hi, wb_lo = split(wbasis_ref[...])
    hi, lo = wb_hi.astype(F32), wb_lo.astype(F32)
    stacked = jnp.concatenate([hi, hi, lo, lo], axis=0).astype(BF16)
    wbt_ref[...] = dot(eye64, stacked, 1, 1).astype(BF16)
    wht_ref[...] = dot(eye64, whid_ref[...], 1, 1).astype(BF16)
    for degree in range(3):
        part = wrad_ref[:, degree * C : degree * C + C]
        wrt_ref[degree * C : degree * C + C, :] = dot(eye, part, 1, 1).astype(BF16)
    wb3_ref[...] = jnp.concatenate([hi, hi, lo], axis=1).astype(BF16)

    base_rows = jnp.broadcast_to(base_ref[...].astype(F32), (128, TILES)).astype(BF16)
    eye_tiles = hot(iota((TILES, TILES), 0) == iota((TILES, TILES), 1))
    base_tiles = dot(eye_tiles, base_rows, 1, 1)
    slots_ref[...] = jnp.where(iota((TILES, EDGE), 0) < live_ref[0, 0], slot_ref[...], RT)
    receiver = base_tiles.astype(I32) + jnp.minimum(slot_ref[...], RT - 1)
    target_ref[...] = receiver

    def place_lanes():
        reach = hot(iota((TILES, JR), 1) // RT == iota((TILES, JR), 0))
        expanded = dot(base_rows, reach, 1, 0).astype(I32) + iota((128, JR), 1) % RT
        return hot(expanded == iota((128, JR), 0))

    def place_rows():
        reach = hot(iota((JR, TILES), 0) // RT == iota((JR, TILES), 1))
        expanded = dot(reach, base_rows, 1, 1).astype(I32) + iota((JR, 128), 0) % RT
        return hot(expanded == iota((JR, 128), 1))

    block_lane = iota((1, 128), 1)
    moved_by = jnp.zeros((1, 128), I32)
    for b in OTHERS:
        offset = 128 * (GROUP[b] + 1) + AT[b] - (ATOMS + b * SLOTS)
        moved_by = jnp.where(block_lane == b + 2, offset, moved_by)
    for g in range(TILES // 8):
        at = slice(8 * g, 8 * g + 8)
        entry = send_ref[at, :]
        entry = entry + lanes(moved_by, jnp.right_shift(entry, 6))
        low_ref[at, :] = jnp.bitwise_and(entry, 127)
        high_ref[at, :] = jnp.right_shift(entry, 7)

    for two in xyz_copies:
        two.wait()
    for d in range(3):
        table_c[0, d : d + 1, :] = own[d : d + 1, :]
    for g, some in enumerate(GROUPS):
        value = in_xyz[some[0], 0:3, :]
        for b in some[1:]:
            value = jnp.where(lane >= AT[b], in_xyz[b, 0:3, :], value)
        table_c[g + 1, 0:3, :] = value

    for g in range(TILES // 8):
        at = slice(8 * g, 8 * g + 8)
        low, high = low_ref[at, :], high_ref[at, :]
        square = None
        for d in range(3):
            value = lanes(table_c[0, d : d + 1, :], low)
            for k in range(1, BLOCKS):
                value = jnp.where(high == k, lanes(table_c[k, d : d + 1, :], low), value)
            u = (value - lanes(own[d : d + 1, :], receiver[at, :])) * INV_CUT
            u_ref[d, at, :] = u
            square = u * u if square is None else square + u * u
        rad_ref[at, :] = square

    for one in row_copies:
        one.wait()
    for k in range(BLOCKS):
        block = table_b[128 * k : 128 * k + 128, :]
        table_t[:, 128 * k : 128 * k + 128] = dot(eye, block, 1, 1).astype(BF16)

    decay = (iota((NB, ES), 0).astype(F32) + 1.0) * 0.5
    slot_ids = iota((RP, PE), 0)
    half_shift = jnp.where(iota((1, PE), 1) < EDGE, 0, RT)
    row_ids = iota((128, PE), 0)

    def tiles_of(ref, first, count):
        return jnp.concatenate([ref[pl.ds(first + k, 1), :] for k in range(count)], axis=1)

    def onehot_of(first):
        pair = tiles_of(slots_ref, first, 2)
        pair = jnp.where(pair < RT, pair + half_shift, RP)
        return jnp.where(slot_ids == pair, 1.0, 0.0)

    def radial_parts(step):
        s = tiles_of(rad_ref, step * TS, TS)
        reach = jnp.maximum(1.0 - s * s, 0.0)
        return s, reach, jnp.exp(-decay * s)

    def forward(step, carry):
        s, reach, fall = radial_parts(step)
        basis = fall * (reach * reach)
        hi = basis.astype(BF16).astype(F32)
        lo = basis - hi
        basis4 = jnp.concatenate([hi, lo, hi, lo], axis=0).astype(BF16)
        pre1 = dot(wbt_ref[...], basis4, 1, 0)
        rows = []
        for q in range(PER_STEP):
            low = tiles_of(low_ref, step * TS + 2 * q, 2)
            high = tiles_of(high_ref, step * TS + 2 * q, 2)
            at_low = hot(row_ids == low)
            total = None
            for k in range(0, BLOCKS, 2):
                both = jnp.concatenate(
                    [at_low * hot(high == k), at_low * hot(high == k + 1)], axis=0
                )
                part = dot(table_t[:, 128 * k : 128 * k + 256], both, 1, 0)
                total = part if total is None else total + part
            rows.append(total)
        sig1 = sigmoid(pre1)
        act1 = pre1 * sig1
        d1_ref[step] = sig1 + act1 * (1.0 - sig1)
        pre2 = dot(wht_ref[...], act1.astype(BF16), 1, 0)
        sig2 = sigmoid(pre2)
        act2 = pre2 * sig2
        d2_ref[step] = sig2 + act2 * (1.0 - sig2)
        act2 = act2.astype(BF16)
        weights = []
        for q in range(PER_STEP):
            first = step * TS + 2 * q
            onehot = onehot_of(first)
            ux, uy, uz = (tiles_of(u_ref.at[d], first, 2) for d in range(3))
            harm = (
                None,
                R3 * ux,
                R3 * uy,
                R3 * uz,
                R15 * ux * uy,
                R15 * uy * uz,
                0.5 * R5 * (2.0 * uz * uz - ux * ux - uy * uy),
                R15 * ux * uz,
                0.5 * R15 * (ux * ux - uy * uy),
            )
            both = jnp.concatenate(
                [onehot if h is None else onehot * h for h in harm], axis=0
            ).astype(BF16)
            a_ref[step * PER_STEP + q] = both
            weights.append(both)
            rows_ref[step * PER_STEP + q] = rows[q]
        for q in range(PER_STEP):
            radial = dot(wrt_ref[...], act2[:, q * PE : q * PE + PE], 1, 0)
            place = pl.ds((step * PER_STEP + q) * RP, RP)
            for degree, (first, last) in enumerate(SPANS):
                g = (radial[degree * C : degree * C + C, :] * rows[q]).astype(BF16)
                g_ref[step * PER_STEP + q, degree * C : degree * C + C, :] = g
                part = dot(weights[q][first * RP : last * RP, :], g, 1, 1).astype(BF16)
                for m in range(first, last):
                    p_ref[place, m * C : m * C + C] = part[
                        (m - first) * RP : (m - first) * RP + RP, :
                    ]
        return carry

    lax.fori_loop(0, STEPS, forward, 0)

    sums = dot(place_lanes(), p_ref[...], 1, 0)
    halves = [0.5 * sums[:, m * C : m * C + C] for m in range(9)]
    inv = [halves[0]]
    for first, last in SPANS[1:]:
        total = halves[first] * halves[first]
        for m in range(first + 1, last):
            total = total + halves[m] * halves[m]
        inv.append(total)
    invariants = jnp.concatenate(inv, axis=1).astype(BF16)
    updated = feat_ref[...].astype(F32) + dot(invariants, wmix_ref[...], 1, 0)
    high = lax.Precision.HIGHEST
    pre = dot(wread_ref[...], updated, 1, 1, high)
    sig = sigmoid(pre)
    act = pre * sig
    row = iota((RO, ATOMS), 0)
    outw = jnp.zeros((RO, ATOMS), F32)
    for r in range(RO):
        outw = jnp.where(row == r, wout_ref[r], outw)
    energy_ref[...] = jnp.sum(outw * act, axis=0, keepdims=True)
    dpre = outw * (sig + act * (1.0 - sig))
    dupd = dot(dpre, wread_ref[...], 0, 0, high)
    dinv = dot(dupd.astype(BF16), wmix_ref[...], 1, 1).astype(BF16).astype(F32)
    grads = []
    for m in range(9):
        part = dinv[:, DEGREE[m] * C : DEGREE[m] * C + C]
        grads.append(0.5 * part if m == 0 else halves[m] * part)
    grads = jnp.concatenate(grads, axis=1).astype(BF16)
    s_ref[...] = dot(place_rows(), grads, 1, 0).astype(BF16)

    def backward(step, carry):
        dradial = []
        for q in range(PER_STEP):
            pair = step * PER_STEP + q
            onehot = onehot_of(step * TS + 2 * q)
            place = pl.ds(pair * RP, RP)
            parts = []
            for degree, (first, last) in enumerate(SPANS):
                cot = jnp.concatenate(
                    [s_ref[place, m * C : m * C + C] for m in range(first, last)], axis=0
                )
                across = slice(degree * C, degree * C + C)
                dg = dot(cot, a_ref[pair, first * RP : last * RP, :], 0, 0)
                parts.append((dg * rows_ref[pair]).astype(BF16))
                if degree:
                    back = dot(cot, g_ref[pair, across, :], 1, 0)
                    for m in range(first, last):
                        one = back[(m - first) * RP : (m - first) * RP + RP, :]
                        dh = jnp.sum(one * onehot, axis=0, keepdims=True)
                        dharm_ref[m, pl.ds(2 * pair, 1), :] = dh[:, 0:EDGE]
                        dharm_ref[m, pl.ds(2 * pair + 1, 1), :] = dh[:, EDGE:PE]
            dradial.append(jnp.concatenate(parts, axis=0))
        dact2 = dot(wrad_ref[...], jnp.concatenate(dradial, axis=1), 1, 0)
        dpre2 = (dact2 * d2_ref[step]).astype(BF16)
        dact1 = dot(whid_ref[...], dpre2, 1, 0)
        dpre1 = dact1 * d1_ref[step]
        hi, lo = split(dpre1)
        dbasis = dot(wb3_ref[...], jnp.concatenate([hi, lo, hi], axis=0), 1, 0)
        s, reach, fall = radial_parts(step)
        slope = fall * (-decay * (reach * reach) - (4.0 * s) * reach)
        ds = jnp.sum(dbasis * slope, axis=0, keepdims=True)
        for k in range(TS):
            drad_ref[pl.ds(step * TS + k, 1), :] = ds[:, k * EDGE : k * EDGE + EDGE]
        return carry

    lax.fori_loop(0, STEPS, backward, 0)

    ux, uy, uz = u_ref[0], u_ref[1], u_ref[2]
    twice = 2.0 * drad_ref[...]
    dh = [None] + [dharm_ref[m] for m in range(1, 9)]
    gx = twice * ux + R3 * dh[1] + R15 * (uy * dh[4] + uz * dh[7] + ux * dh[8]) - R5 * (ux * dh[6])
    gy = twice * uy + R3 * dh[2] + R15 * (ux * dh[4] + uz * dh[5] - uy * dh[8]) - R5 * (uy * dh[6])
    gz = twice * uz + R3 * dh[3] + R15 * (uy * dh[5] + ux * dh[7]) + (2.0 * R5) * (uz * dh[6])
    gsep_ref[0] = gx * INV_CUT
    gsep_ref[1] = gy * INV_CUT
    gsep_ref[2] = gz * INV_CUT

    acc_ref[...] = jnp.zeros_like(acc_ref)
    racc_ref[...] = jnp.zeros_like(racc_ref)

    def scatter(step, carry):
        for q in range(PER_STEP):
            first = step * TS + 2 * q
            at_low = hot(row_ids == tiles_of(low_ref, first, 2))
            at_target = hot(row_ids == tiles_of(target_ref, first, 2))
            at_high = iota((8, PE), 0) == tiles_of(high_ref, first, 2)
            left, flat = [], []
            for d in range(3):
                g = tiles_of(gsep_ref.at[d], first, 2)
                hi = g.astype(BF16).astype(F32)
                lo = g - hi
                left += [jnp.where(at_high, hi, 0.0), jnp.where(at_high, lo, 0.0)]
                flat += [hi, lo]
            left = jnp.concatenate(left, axis=0).astype(BF16)
            row8 = iota((8, PE), 0)
            stack = jnp.zeros((8, PE), F32)
            for k, value in enumerate(flat):
                stack = jnp.where(row8 == k, value, stack)
            acc_ref[...] += dot(left, at_low, 1, 1)
            racc_ref[...] += dot(stack.astype(BF16), at_target, 1, 1)
        return carry

    lax.fori_loop(0, STEPS, scatter, 0)

    for d in range(3):
        grid = acc_ref[16 * d : 16 * d + 8, :] + acc_ref[16 * d + 8 : 16 * d + 16, :]
        for g in range(NG):
            out_grad[g, d : d + 1, :] = grid[g + 1 : g + 2, :]
        mine = racc_ref[2 * d : 2 * d + 1, :] + racc_ref[2 * d + 1 : 2 * d + 2, :]
        force_ref[d] = mine - grid[0:1, :]

    grad_copies = []
    for b in OTHERS:
        copy = pltpu.make_async_remote_copy(
            src_ref=out_grad.at[GROUP[b]],
            dst_ref=in_grad.at[26 - b],
            send_sem=grad_send.at[b],
            recv_sem=grad_recv.at[26 - b],
            device_id=device(b),
            device_id_type=MESH,
        )
        copy.start()
        grad_copies.append(copy)
    for copy in grad_copies:
        copy.wait()

    total = jnp.zeros((8, ATOMS), F32)
    row8 = iota((8, 128), 0)
    for g, some in enumerate(GROUPS):
        order = sorted(some, key=lambda b: AT[26 - b])
        came = in_grad[order[0]]
        for b in order[1:]:
            came = jnp.where(lane >= AT[26 - b], in_grad[b], came)
        hi, lo = split(jnp.where(row8 < 3, came, 0.0))
        total = total + dot(hi, chosen_ref[g], 1, 1) + dot(lo, chosen_ref[g], 1, 1)
    for d in range(3):
        force_ref[d] = force_ref[d] - total[d : d + 1, :]


def solution(mesh):
    sizes = tuple(mesh.shape[name] for name in ("gx", "gy", "gz"))
    vmem = pl.BlockSpec(memory_space=pltpu.VMEM)
    hbm = pl.BlockSpec(memory_space=pltpu.HBM)
    pairs = TILES // 2

    def step(
        features,
        positions,
        w_up,
        w_basis,
        w_hidden,
        w_radial,
        w_mix,
        w_read,
        w_out,
        send_lists,
        tile_senders,
        tile_slots,
        tile_bases,
        tile_live,
    ):
        dma = pltpu.SemaphoreType.DMA((27,))
        force, energy = pl.pallas_call(
            functools.partial(kernel, sizes),
            out_shape=(
                jax.ShapeDtypeStruct((3, 1, ATOMS), F32),
                jax.ShapeDtypeStruct((1, ATOMS), F32),
            ),
            in_specs=[hbm] * 14,
            out_specs=(vmem, vmem),
            scratch_shapes=[
                pltpu.VMEM((ATOMS, C), BF16),
                pltpu.VMEM((3, 1, ATOMS), F32),
                pltpu.VMEM((C, C), BF16),
                pltpu.VMEM((NB, RH), F32),
                pltpu.VMEM((RH, RH), BF16),
                pltpu.VMEM((RH, 3 * C), BF16),
                pltpu.VMEM((3 * C, C), BF16),
                pltpu.VMEM((RO, C), F32),
                pltpu.SMEM((RO,), F32),
                pltpu.VMEM((27, 1, SLOTS), I32),
                pltpu.VMEM((TILES, EDGE), I32),
                pltpu.VMEM((TILES, EDGE), I32),
                pltpu.VMEM((1, TILES), I32),
                pltpu.SMEM((1, 1), I32),
                pltpu.SemaphoreType.DMA((14,)),
                pltpu.VMEM((NG * 128, C), BF16),
                pltpu.VMEM((NG, 8, 128), F32),
                pltpu.VMEM((BLOCKS * 128, C), BF16),
                pltpu.VMEM((27, 8, 128), F32),
                pltpu.VMEM((C, BLOCKS * 128), BF16),
                pltpu.VMEM((BLOCKS, 8, 128), F32),
                pltpu.VMEM((NG, ATOMS, 128), BF16),
                pltpu.VMEM((pairs, C, PE), F32),
                pltpu.VMEM((pairs, 3 * C, PE), BF16),
                pltpu.VMEM((pairs, 9 * RP, PE), BF16),
                pltpu.VMEM((STEPS, RH, ES), F32),
                pltpu.VMEM((STEPS, RH, ES), F32),
                pltpu.VMEM((JR, 9 * C), BF16),
                pltpu.VMEM((JR, 9 * C), BF16),
                pltpu.VMEM((3, TILES, EDGE), F32),
                pltpu.VMEM((TILES, EDGE), F32),
                pltpu.VMEM((TILES, EDGE), I32),
                pltpu.VMEM((TILES, EDGE), I32),
                pltpu.VMEM((TILES, EDGE), I32),
                pltpu.VMEM((TILES, EDGE), I32),
                pltpu.VMEM((9, TILES, EDGE), F32),
                pltpu.VMEM((TILES, EDGE), F32),
                pltpu.VMEM((3, TILES, EDGE), F32),
                pltpu.VMEM((48, 128), F32),
                pltpu.VMEM((8, 128), F32),
                pltpu.VMEM((NG, 8, 128), F32),
                pltpu.VMEM((27, 8, 128), F32),
                pltpu.VMEM((RH, 4 * NB), BF16),
                pltpu.VMEM((RH, RH), BF16),
                pltpu.VMEM((3 * C, RH), BF16),
                pltpu.VMEM((NB, 3 * RH), BF16),
                dma,
                dma,
                dma,
                dma,
                dma,
                dma,
            ],
            compiler_params=pltpu.CompilerParams(
                collective_id=0,
                has_side_effects=True,
                vmem_limit_bytes=64 * 2**20 - 65536,
            ),
        )(
            features.reshape(ATOMS, C),
            positions.reshape(3, 1, ATOMS),
            w_up,
            w_basis,
            w_hidden,
            w_radial,
            w_mix,
            w_read.T,
            w_out,
            send_lists.reshape(27, 1, SLOTS),
            tile_senders.reshape(TILES, EDGE),
            tile_slots.reshape(TILES, EDGE),
            tile_bases.reshape(1, TILES),
            tile_live.reshape(1, 1),
        )
        return force.reshape(1, 1, 1, 3, ATOMS), energy.reshape(1, 1, 1, ATOMS)

    cube = ("gx", "gy", "gz")
    return jax.shard_map(
        step,
        mesh=mesh,
        in_specs=(
            P(*cube, None, None),
            P(*cube, None, None),
            P(),
            P(),
            P(),
            P(),
            P(),
            P(),
            P(),
            P(*cube, None, None, None, None),
            P(*cube, None, None),
            P(*cube, None, None),
            P(*cube, None),
            P(*cube),
        ),
        out_specs=(P(*cube, None, None), P(*cube, None)),
        check_vma=False,
    )
```

```python
import functools

import jax
import jax.numpy as jnp
from jax import lax
from jax.experimental import pallas as pl
from jax.experimental.pallas import tpu as pltpu
from jax.sharding import PartitionSpec as P

MESH = pl.DeviceIdType.MESH
F32 = jnp.float32
BF16 = jnp.bfloat16
I32 = jnp.int32

ATOMS = 128
C = 128
SLOTS = 64
TILES = 64
EDGE = 128
RT = 8
RH = 64
NB = 8
RO = 16
JR = TILES * RT
PE = 2 * EDGE
RP = 2 * RT
PER_STEP = 4
STEPS = TILES // 2 // PER_STEP
ES = PE * PER_STEP
TS = 2 * PER_STEP

SIDE = 11.0
INV_CUT = 0.2
R3 = 3.0**0.5
R5 = 5.0**0.5
R15 = 15.0**0.5
DEGREE = (0, 1, 1, 1, 2, 2, 2, 2, 2)
SPANS = ((0, 1), (1, 4), (4, 9))

DIRS = tuple((b // 9 - 1, b // 3 % 3 - 1, b % 3 - 1) for b in range(27))
NONZERO = tuple(sum(v != 0 for v in d) for d in DIRS)
COUNT = tuple(SLOTS * 2 // 2 ** max(k, 1) for k in NONZERO)
OTHERS = tuple(b for b in range(27) if b != 13)


def groups_of():
    groups = []
    for k in (1, 2, 3):
        here = [b for b in OTHERS if NONZERO[b] == k and b < 13]
        per = ATOMS // (SLOTS * 2 // 2**k) // 2
        for first in range(0, len(here), per):
            some = here[first : first + per]
            groups.append(tuple(some) + tuple(26 - b for b in some))
    return tuple(groups)


GROUPS = groups_of()
NG = len(GROUPS)
BLOCKS = NG + 1
GROUP = {b: g for g, some in enumerate(GROUPS) for b in some}
AT = {b: k * COUNT[b] for some in GROUPS for k, b in enumerate(some)}


def dot(a, b, ca, cb, precision=None):
    return lax.dot_general(
        a, b, (((ca,), (cb,)), ((), ())), preferred_element_type=F32, precision=precision
    )


def iota(shape, dim):
    return lax.broadcasted_iota(I32, shape, dim)


def hot(condition):
    return jnp.where(condition, 1.0, 0.0).astype(BF16)


def sigmoid(x):
    return 0.5 + 0.5 * jnp.tanh(0.5 * x)


def split(x):
    hi = x.astype(BF16)
    return hi, (x - hi.astype(F32)).astype(BF16)


def lanes(row, index):
    return jnp.take_along_axis(jnp.broadcast_to(row, index.shape), index, axis=1)


def kernel(
    sizes,
    feat_hbm,
    pos_hbm,
    wup_hbm,
    wbasis_hbm,
    whid_hbm,
    wrad_hbm,
    wmix_hbm,
    wread_hbm,
    wout_hbm,
    lists_hbm,
    send_hbm,
    slot_hbm,
    base_hbm,
    live_hbm,
    force_ref,
    energy_ref,
    feat_ref,
    pos_ref,
    wup_ref,
    wbasis_ref,
    whid_ref,
    wrad_ref,
    wmix_ref,
    wread_ref,
    wout_ref,
    lists_ref,
    send_ref,
    slot_ref,
    base_ref,
    live_ref,
    stage_sem,
    out_rows,
    out_xyz,
    table_b,
    in_xyz,
    table_t,
    table_c,
    chosen_ref,
    at_ref,
    h2_ref,
    rows_ref,
    g_ref,
    dr_ref,
    a_ref,
    d1_ref,
    d2_ref,
    p_ref,
    s_ref,
    u_ref,
    rad_ref,
    harm_ref,
    slots_ref,
    low_ref,
    high_ref,
    target_ref,
    dharm_ref,
    drad_ref,
    gsep_ref,
    acc_ref,
    racc_ref,
    out_grad,
    in_grad,
    wbt_ref,
    wht_ref,
    wrt_ref,
    wb3_ref,
    row_send,
    row_recv,
    xyz_send,
    xyz_recv,
    grad_send,
    grad_recv,
):
    here = tuple(lax.axis_index(name) for name in ("gx", "gy", "gz"))

    def device(b):
        return tuple(lax.rem(c + (d + n), n) for c, d, n in zip(here, DIRS[b], sizes))

    barrier = pltpu.get_barrier_semaphore()
    for b in OTHERS:
        pl.semaphore_signal(barrier, inc=1, device_id=device(b), device_id_type=MESH)

    staged = {}
    moves = (
        ("feat", feat_hbm, feat_ref),
        ("wup", wup_hbm, wup_ref),
        ("lists", lists_hbm, lists_ref),
        ("pos", pos_hbm, pos_ref),
        ("base", base_hbm, base_ref),
        ("live", live_hbm, live_ref),
        ("slot", slot_hbm, slot_ref),
        ("send", send_hbm, send_ref),
        ("wbasis", wbasis_hbm, wbasis_ref),
        ("whid", whid_hbm, whid_ref),
        ("wrad", wrad_hbm, wrad_ref),
        ("wmix", wmix_hbm, wmix_ref),
        ("wread", wread_hbm, wread_ref),
        ("wout", wout_hbm, wout_ref),
    )
    for k, (name, source, target) in enumerate(moves):
        staged[name] = pltpu.make_async_copy(source, target, stage_sem.at[k])
        staged[name].start()
    early = ("feat", "wup", "lists", "pos")
    for name in early:
        staged[name].wait()

    projected = dot(feat_ref[...], wup_ref[...], 1, 0).astype(BF16)
    table_b[0:ATOMS, :] = projected
    own = jnp.concatenate([pos_ref[d] for d in range(3)], axis=0)
    lane = iota((1, 128), 1)
    for g, some in enumerate(GROUPS):
        order = sorted(some, key=lambda b: AT[26 - b])
        named = jnp.concatenate([lists_ref[b][:, 0 : COUNT[b]] for b in order], axis=1)
        chosen = hot(iota((ATOMS, 128), 0) == named)
        chosen_ref[g] = chosen
        out_rows[128 * g : 128 * g + 128, :] = dot(chosen, projected, 0, 0).astype(BF16)
        for d in range(3):
            shift = jnp.zeros((1, 128), F32)
            for b in some:
                if DIRS[b][d]:
                    inside = (lane >= AT[26 - b]) & (lane < AT[26 - b] + COUNT[b])
                    shift = jnp.where(inside, -SIDE * DIRS[b][d], shift)
            moved = lanes(own[d : d + 1, :], jnp.broadcast_to(named, (8, 128)))[0:1, :]
            out_xyz[g, d : d + 1, :] = moved + shift

    pl.semaphore_wait(barrier, 26)

    row_copies, xyz_copies = [], []
    for b in OTHERS:
        n, g, spot = COUNT[b], GROUP[b], AT[26 - b]
        row_copies.append(
            pltpu.make_async_remote_copy(
                src_ref=out_rows.at[pl.ds(128 * g + spot, n), :],
                dst_ref=table_b.at[pl.ds(128 * (g + 1) + spot, n), :],
                send_sem=row_send.at[b],
                recv_sem=row_recv.at[26 - b],
                device_id=device(b),
                device_id_type=MESH,
            )
        )
        xyz_copies.append(
            pltpu.make_async_remote_copy(
                src_ref=out_xyz.at[g],
                dst_ref=in_xyz.at[26 - b],
                send_sem=xyz_send.at[b],
                recv_sem=xyz_recv.at[26 - b],
                device_id=device(b),
                device_id_type=MESH,
            )
        )
    for one, two in zip(row_copies, xyz_copies):
        two.start()
        one.start()

    for name in staged:
        if name not in early:
            staged[name].wait()

    eye = hot(iota((128, 128), 0) == iota((128, 128), 1))
    eye64 = eye[0:64, 0:64]
    wb_hi, wb_lo = split(wbasis_ref[...])
    hi, lo = wb_hi.astype(F32), wb_lo.astype(F32)
    stacked = jnp.concatenate([hi, hi, lo, lo], axis=0).astype(BF16)
    wbt_ref[...] = dot(eye64, stacked, 1, 1).astype(BF16)
    wht_ref[...] = dot(eye64, whid_ref[...], 1, 1).astype(BF16)
    for degree in range(3):
        part = wrad_ref[:, degree * C : degree * C + C]
        wrt_ref[degree * C : degree * C + C, :] = dot(eye, part, 1, 1).astype(BF16)
    wb3_ref[...] = jnp.concatenate([hi, hi, lo], axis=1).astype(BF16)

    base_rows = jnp.broadcast_to(base_ref[...].astype(F32), (128, TILES)).astype(BF16)
    eye_tiles = hot(iota((TILES, TILES), 0) == iota((TILES, TILES), 1))
    base_tiles = dot(eye_tiles, base_rows, 1, 1)
    slots_ref[...] = jnp.where(iota((TILES, EDGE), 0) < live_ref[0, 0], slot_ref[...], RT)
    receiver = base_tiles.astype(I32) + jnp.minimum(slot_ref[...], RT - 1)
    target_ref[...] = receiver

    def place_lanes():
        reach = hot(iota((TILES, JR), 1) // RT == iota((TILES, JR), 0))
        expanded = dot(base_rows, reach, 1, 0).astype(I32) + iota((128, JR), 1) % RT
        return hot(expanded == iota((128, JR), 0))

    def place_rows():
        reach = hot(iota((JR, TILES), 0) // RT == iota((JR, TILES), 1))
        expanded = dot(reach, base_rows, 1, 1).astype(I32) + iota((JR, 128), 0) % RT
        return hot(expanded == iota((JR, 128), 1))

    block_lane = iota((1, 128), 1)
    moved_by = jnp.zeros((1, 128), I32)
    for b in OTHERS:
        offset = 128 * (GROUP[b] + 1) + AT[b] - (ATOMS + b * SLOTS)
        moved_by = jnp.where(block_lane == b + 2, offset, moved_by)
    for g in range(TILES // 8):
        at = slice(8 * g, 8 * g + 8)
        entry = send_ref[at, :]
        entry = entry + lanes(moved_by, jnp.right_shift(entry, 6))
        low_ref[at, :] = jnp.bitwise_and(entry, 127)
        high_ref[at, :] = jnp.right_shift(entry, 7)

    for two in xyz_copies:
        two.wait()
    for d in range(3):
        table_c[0, d : d + 1, :] = own[d : d + 1, :]
    for g, some in enumerate(GROUPS):
        value = in_xyz[some[0], 0:3, :]
        for b in some[1:]:
            value = jnp.where(lane >= AT[b], in_xyz[b, 0:3, :], value)
        table_c[g + 1, 0:3, :] = value

    for g in range(TILES // 8):
        at = slice(8 * g, 8 * g + 8)
        low, high = low_ref[at, :], high_ref[at, :]
        parts = []
        for d in range(3):
            value = lanes(table_c[0, d : d + 1, :], low)
            for k in range(1, BLOCKS):
                value = jnp.where(high == k, lanes(table_c[k, d : d + 1, :], low), value)
            u = (value - lanes(own[d : d + 1, :], receiver[at, :])) * INV_CUT
            u_ref[d, at, :] = u
            parts.append(u)
        ux, uy, uz = parts
        xx, yy, zz = ux * ux, uy * uy, uz * uz
        rad_ref[at, :] = xx + yy + zz
        values = (
            R3 * ux,
            R3 * uy,
            R3 * uz,
            R15 * ux * uy,
            R15 * uy * uz,
            0.5 * R5 * (2.0 * zz - xx - yy),
            R15 * ux * uz,
            0.5 * R15 * (xx - yy),
        )
        for m, value in enumerate(values):
            harm_ref[m, at, :] = value

    for one in row_copies:
        one.wait()
    for k in range(BLOCKS):
        block = table_b[128 * k : 128 * k + 128, :]
        table_t[:, 128 * k : 128 * k + 128] = dot(eye, block, 1, 1).astype(BF16)

    decay = (iota((NB, PE), 0).astype(F32) + 1.0) * 0.5
    slot_ids = iota((RP, PE), 0)
    half_shift = jnp.where(iota((1, PE), 1) < EDGE, 0, RT)
    row_ids = iota((128, PE), 0)
    inner = range(PER_STEP)

    def tiles_of(ref, first, count):
        return jnp.concatenate([ref[pl.ds(first + k, 1), :] for k in range(count)], axis=1)

    def onehot_of(first):
        pair = tiles_of(slots_ref, first, 2)
        pair = jnp.where(pair < RT, pair + half_shift, RP)
        return jnp.where(slot_ids == pair, 1.0, 0.0)

    def radial_parts(pair):
        s = tiles_of(rad_ref, 2 * pair, 2)
        reach = jnp.maximum(1.0 - s * s, 0.0)
        return s, reach, jnp.exp(-decay * s)

    def gather(pair):
        low = tiles_of(low_ref, 2 * pair, 2)
        high = tiles_of(high_ref, 2 * pair, 2)
        at_low = hot(row_ids == low)
        at_ref[pair] = at_low
        entries = jnp.concatenate([at_low * hot(high == k) for k in range(BLOCKS)], axis=0)
        rows_ref[pair] = dot(table_t[...], entries, 1, 0).astype(BF16)

    def network(step):
        pairs = [step * PER_STEP + q for q in inner]
        basis4 = []
        for pair in pairs:
            s, reach, fall = radial_parts(pair)
            basis = fall * (reach * reach)
            hi = basis.astype(BF16).astype(F32)
            lo = basis - hi
            basis4.append(jnp.concatenate([hi, lo, hi, lo], axis=0).astype(BF16))
        pre1 = [dot(wbt_ref[...], value, 1, 0) for value in basis4]
        for pair in pairs[: PER_STEP // 2]:
            gather(pair)
        act1 = []
        for pair, pre in zip(pairs, pre1):
            sig = sigmoid(pre)
            act = pre * sig
            d1_ref[pair] = sig + act * (1.0 - sig)
            act1.append(act.astype(BF16))
        pre2 = [dot(wht_ref[...], value, 1, 0) for value in act1]
        for pair in pairs[PER_STEP // 2 :]:
            gather(pair)
        for pair, pre in zip(pairs, pre2):
            sig = sigmoid(pre)
            act = pre * sig
            d2_ref[pair] = sig + act * (1.0 - sig)
            h2_ref[pair] = act.astype(BF16)

    def gathered(step):
        for q in inner:
            pair = step * PER_STEP + q
            onehot = onehot_of(2 * pair)
            weights = [onehot]
            for m in range(8):
                weights.append(onehot * tiles_of(harm_ref.at[m], 2 * pair, 2))
            weights = jnp.concatenate(weights, axis=0).astype(BF16)
            a_ref[pair] = weights
            rows = rows_ref[pair]
            place = pl.ds(pair * RP, RP)
            radial = dot(wrt_ref[...], h2_ref[pair], 1, 0).astype(BF16)
            for degree, (first, last) in enumerate(SPANS):
                across = slice(degree * C, degree * C + C)
                g = radial[across, :] * rows
                g_ref[pair, across, :] = g
                part = dot(weights[first * RP : last * RP, :], g, 1, 1).astype(BF16)
                for m in range(first, last):
                    p_ref[place, m * C : m * C + C] = part[
                        (m - first) * RP : (m - first) * RP + RP, :
                    ]

    def forward(step, carry):
        gathered(lax.rem(step + (STEPS - 1), STEPS))
        network(step)
        return carry

    lax.fori_loop(0, STEPS, forward, 0)
    gathered(STEPS - 1)

    sums = dot(place_lanes(), p_ref[...], 1, 0)
    halves = [0.5 * sums[:, m * C : m * C + C] for m in range(9)]
    inv = [halves[0]]
    for first, last in SPANS[1:]:
        total = halves[first] * halves[first]
        for m in range(first + 1, last):
            total = total + halves[m] * halves[m]
        inv.append(total)
    invariants = jnp.concatenate(inv, axis=1).astype(BF16)
    updated = feat_ref[...].astype(F32) + dot(invariants, wmix_ref[...], 1, 0)
    high = lax.Precision.HIGHEST
    pre = dot(wread_ref[...], updated, 1, 1, high)
    sig = sigmoid(pre)
    act = pre * sig
    row = iota((RO, ATOMS), 0)
    outw = jnp.zeros((RO, ATOMS), F32)
    for r in range(RO):
        outw = jnp.where(row == r, wout_ref[r], outw)
    energy_ref[...] = jnp.sum(outw * act, axis=0, keepdims=True)
    dpre = outw * (sig + act * (1.0 - sig))
    dupd = dot(dpre, wread_ref[...], 0, 0, high)
    dinv = dot(dupd.astype(BF16), wmix_ref[...], 1, 1).astype(BF16).astype(F32)
    grads = []
    for m in range(9):
        part = dinv[:, DEGREE[m] * C : DEGREE[m] * C + C]
        grads.append(0.5 * part if m == 0 else halves[m] * part)
    grads = jnp.concatenate(grads, axis=1).astype(BF16)
    s_ref[...] = dot(place_rows(), grads, 1, 0).astype(BF16)

    acc_ref[...] = jnp.zeros_like(acc_ref)
    racc_ref[...] = jnp.zeros_like(racc_ref)

    def to_edges(step):
        for q in inner:
            pair = step * PER_STEP + q
            onehot = onehot_of(2 * pair)
            place = pl.ds(pair * RP, RP)
            rows = rows_ref[pair]
            for degree, (first, last) in enumerate(SPANS):
                cot = jnp.concatenate(
                    [s_ref[place, m * C : m * C + C] for m in range(first, last)], axis=0
                )
                across = slice(degree * C, degree * C + C)
                dg = dot(cot, a_ref[pair, first * RP : last * RP, :], 0, 0)
                dr_ref[pair, across, :] = dg.astype(BF16) * rows
                if degree:
                    back = dot(cot, g_ref[pair, across, :], 1, 0)
                    for m in range(first, last):
                        one = back[(m - first) * RP : (m - first) * RP + RP, :]
                        dh = jnp.sum(one * onehot, axis=0, keepdims=True)
                        dharm_ref[m, pl.ds(2 * pair, 1), :] = dh[:, 0:EDGE]
                        dharm_ref[m, pl.ds(2 * pair + 1, 1), :] = dh[:, EDGE:PE]

    def to_radius(step):
        pairs = [step * PER_STEP + q for q in inner]
        dact2 = [dot(wrad_ref[...], dr_ref[pair], 1, 0) for pair in pairs]
        dpre2 = [(value * d2_ref[pair]).astype(BF16) for value, pair in zip(dact2, pairs)]
        dact1 = [dot(whid_ref[...], value, 1, 0) for value in dpre2]
        stacks = []
        for value, pair in zip(dact1, pairs):
            hi, lo = split(value * d1_ref[pair])
            stacks.append(jnp.concatenate([hi, lo, hi], axis=0))
        dbasis = [dot(wb3_ref[...], value, 1, 0) for value in stacks]
        for value, pair in zip(dbasis, pairs):
            s, reach, fall = radial_parts(pair)
            slope = fall * (-decay * (reach * reach) - (4.0 * s) * reach)
            ds = jnp.sum(value * slope, axis=0, keepdims=True)
            drad_ref[pl.ds(2 * pair, 1), :] = ds[:, 0:EDGE]
            drad_ref[pl.ds(2 * pair + 1, 1), :] = ds[:, EDGE:PE]

    def scatter(step, counts):
        at = pl.ds(pl.multiple_of(step * TS, TS), TS)
        ux, uy, uz = u_ref[0, at, :], u_ref[1, at, :], u_ref[2, at, :]
        twice = 2.0 * drad_ref[at, :]
        dh = [None] + [dharm_ref[m, at, :] for m in range(1, 9)]
        gx = R3 * dh[1] + R15 * (uy * dh[4] + uz * dh[7] + ux * dh[8]) - R5 * (ux * dh[6])
        gy = R3 * dh[2] + R15 * (ux * dh[4] + uz * dh[5] - uy * dh[8]) - R5 * (uy * dh[6])
        gz = R3 * dh[3] + R15 * (uy * dh[5] + ux * dh[7]) + (2.0 * R5) * (uz * dh[6])
        for d, value in enumerate((twice * ux + gx, twice * uy + gy, twice * uz + gz)):
            g = jnp.where(counts, value * INV_CUT, 0.0)
            hi = g.astype(BF16).astype(F32)
            gsep_ref[2 * d] = hi
            gsep_ref[2 * d + 1] = g - hi
        at_high = iota((8, ES), 0) == tiles_of(high_ref, step * TS, TS)
        at_target = hot(iota((128, ES), 0) == tiles_of(target_ref, step * TS, TS))
        at_low = jnp.concatenate([at_ref[step * PER_STEP + q] for q in inner], axis=1)
        row8 = iota((8, ES), 0)
        left, stack = [], jnp.zeros((8, ES), F32)
        for k in range(6):
            value = tiles_of(gsep_ref.at[k], 0, TS)
            left.append(jnp.where(at_high, value, 0.0))
            stack = jnp.where(row8 == k, value, stack)
        acc_ref[...] += dot(jnp.concatenate(left, axis=0).astype(BF16), at_low, 1, 1)
        racc_ref[...] += dot(stack.astype(BF16), at_target, 1, 1)

    def backward(step, carry):
        scatter(lax.rem(step + (STEPS - 2), STEPS), step >= 2)
        to_radius(lax.rem(step + (STEPS - 1), STEPS))
        to_edges(step)
        return carry

    lax.fori_loop(0, STEPS, backward, 0)
    scatter(STEPS - 2, True)
    to_radius(STEPS - 1)
    scatter(STEPS - 1, True)

    for d in range(3):
        grid = acc_ref[16 * d : 16 * d + 8, :] + acc_ref[16 * d + 8 : 16 * d + 16, :]
        for g in range(NG):
            out_grad[g, d : d + 1, :] = grid[g + 1 : g + 2, :]
        mine = racc_ref[2 * d : 2 * d + 1, :] + racc_ref[2 * d + 1 : 2 * d + 2, :]
        force_ref[d] = mine - grid[0:1, :]

    grad_copies = []
    for b in OTHERS:
        copy = pltpu.make_async_remote_copy(
            src_ref=out_grad.at[GROUP[b]],
            dst_ref=in_grad.at[26 - b],
            send_sem=grad_send.at[b],
            recv_sem=grad_recv.at[26 - b],
            device_id=device(b),
            device_id_type=MESH,
        )
        copy.start()
        grad_copies.append(copy)
    for copy in grad_copies:
        copy.wait()

    total = jnp.zeros((8, ATOMS), F32)
    row8 = iota((8, 128), 0)
    for g, some in enumerate(GROUPS):
        order = sorted(some, key=lambda b: AT[26 - b])
        came = in_grad[order[0]]
        for b in order[1:]:
            came = jnp.where(lane >= AT[26 - b], in_grad[b], came)
        hi, lo = split(jnp.where(row8 < 3, came, 0.0))
        total = total + dot(hi, chosen_ref[g], 1, 1) + dot(lo, chosen_ref[g], 1, 1)
    for d in range(3):
        force_ref[d] = force_ref[d] - total[d : d + 1, :]


def solution(mesh):
    sizes = tuple(mesh.shape[name] for name in ("gx", "gy", "gz"))
    vmem = pl.BlockSpec(memory_space=pltpu.VMEM)
    hbm = pl.BlockSpec(memory_space=pltpu.HBM)
    pairs = TILES // 2

    def step(
        features,
        positions,
        w_up,
        w_basis,
        w_hidden,
        w_radial,
        w_mix,
        w_read,
        w_out,
        send_lists,
        tile_senders,
        tile_slots,
        tile_bases,
        tile_live,
    ):
        dma = pltpu.SemaphoreType.DMA((27,))
        force, energy = pl.pallas_call(
            functools.partial(kernel, sizes),
            out_shape=(
                jax.ShapeDtypeStruct((3, 1, ATOMS), F32),
                jax.ShapeDtypeStruct((1, ATOMS), F32),
            ),
            in_specs=[hbm] * 14,
            out_specs=(vmem, vmem),
            scratch_shapes=[
                pltpu.VMEM((ATOMS, C), BF16),
                pltpu.VMEM((3, 1, ATOMS), F32),
                pltpu.VMEM((C, C), BF16),
                pltpu.VMEM((NB, RH), F32),
                pltpu.VMEM((RH, RH), BF16),
                pltpu.VMEM((RH, 3 * C), BF16),
                pltpu.VMEM((3 * C, C), BF16),
                pltpu.VMEM((RO, C), F32),
                pltpu.SMEM((RO,), F32),
                pltpu.VMEM((27, 1, SLOTS), I32),
                pltpu.VMEM((TILES, EDGE), I32),
                pltpu.VMEM((TILES, EDGE), I32),
                pltpu.VMEM((1, TILES), I32),
                pltpu.SMEM((1, 1), I32),
                pltpu.SemaphoreType.DMA((14,)),
                pltpu.VMEM((NG * 128, C), BF16),
                pltpu.VMEM((NG, 8, 128), F32),
                pltpu.VMEM((BLOCKS * 128, C), BF16),
                pltpu.VMEM((27, 8, 128), F32),
                pltpu.VMEM((C, BLOCKS * 128), BF16),
                pltpu.VMEM((BLOCKS, 8, 128), F32),
                pltpu.VMEM((NG, ATOMS, 128), BF16),
                pltpu.VMEM((pairs, 128, PE), BF16),
                pltpu.VMEM((pairs, RH, PE), BF16),
                pltpu.VMEM((pairs, C, PE), BF16),
                pltpu.VMEM((pairs, 3 * C, PE), BF16),
                pltpu.VMEM((pairs, 3 * C, PE), BF16),
                pltpu.VMEM((pairs, 9 * RP, PE), BF16),
                pltpu.VMEM((pairs, RH, PE), F32),
                pltpu.VMEM((pairs, RH, PE), F32),
                pltpu.VMEM((JR, 9 * C), BF16),
                pltpu.VMEM((JR, 9 * C), BF16),
                pltpu.VMEM((3, TILES, EDGE), F32),
                pltpu.VMEM((TILES, EDGE), F32),
                pltpu.VMEM((8, TILES, EDGE), F32),
                pltpu.VMEM((TILES, EDGE), I32),
                pltpu.VMEM((TILES, EDGE), I32),
                pltpu.VMEM((TILES, EDGE), I32),
                pltpu.VMEM((TILES, EDGE), I32),
                pltpu.VMEM((9, TILES, EDGE), F32),
                pltpu.VMEM((TILES, EDGE), F32),
                pltpu.VMEM((6, TS, EDGE), F32),
                pltpu.VMEM((48, 128), F32),
                pltpu.VMEM((8, 128), F32),
                pltpu.VMEM((NG, 8, 128), F32),
                pltpu.VMEM((27, 8, 128), F32),
                pltpu.VMEM((RH, 4 * NB), BF16),
                pltpu.VMEM((RH, RH), BF16),
                pltpu.VMEM((3 * C, RH), BF16),
                pltpu.VMEM((NB, 3 * RH), BF16),
                dma,
                dma,
                dma,
                dma,
                dma,
                dma,
            ],
            compiler_params=pltpu.CompilerParams(
                collective_id=0,
                has_side_effects=True,
                vmem_limit_bytes=64 * 2**20 - 65536,
            ),
        )(
            features.reshape(ATOMS, C),
            positions.reshape(3, 1, ATOMS),
            w_up,
            w_basis,
            w_hidden,
            w_radial,
            w_mix,
            w_read.T,
            w_out,
            send_lists.reshape(27, 1, SLOTS),
            tile_senders.reshape(TILES, EDGE),
            tile_slots.reshape(TILES, EDGE),
            tile_bases.reshape(1, TILES),
            tile_live.reshape(1, 1),
        )
        return force.reshape(1, 1, 1, 3, ATOMS), energy.reshape(1, 1, 1, ATOMS)

    cube = ("gx", "gy", "gz")
    return jax.shard_map(
        step,
        mesh=mesh,
        in_specs=(
            P(*cube, None, None),
            P(*cube, None, None),
            P(),
            P(),
            P(),
            P(),
            P(),
            P(),
            P(),
            P(*cube, None, None, None, None),
            P(*cube, None, None),
            P(*cube, None, None),
            P(*cube, None),
            P(*cube),
        ),
        out_specs=(P(*cube, None, None), P(*cube, None)),
        check_vma=False,
    )
```

```python
import functools

import jax
import jax.numpy as jnp
from jax import lax
from jax.experimental import pallas as pl
from jax.experimental.pallas import tpu as pltpu
from jax.sharding import PartitionSpec as P

MESH = pl.DeviceIdType.MESH
F32 = jnp.float32
BF16 = jnp.bfloat16
I32 = jnp.int32

ATOMS = 128
C = 128
SLOTS = 64
TILES = 64
EDGE = 128
RT = 8
RH = 64
NB = 8
RO = 16
JR = TILES * RT
PE = 2 * EDGE
RP = 2 * RT
PER_STEP = 4
STEPS = TILES // 2 // PER_STEP
ES = PE * PER_STEP
NETWORK = 8
TS = 2 * PER_STEP

SIDE = 11.0
INV_CUT = 0.2
R3 = 3.0**0.5
R5 = 5.0**0.5
R15 = 15.0**0.5
DEGREE = (0, 1, 1, 1, 2, 2, 2, 2, 2)
SPANS = ((0, 1), (1, 4), (4, 9))

DIRS = tuple((b // 9 - 1, b // 3 % 3 - 1, b % 3 - 1) for b in range(27))
NONZERO = tuple(sum(v != 0 for v in d) for d in DIRS)
COUNT = tuple(SLOTS * 2 // 2 ** max(k, 1) for k in NONZERO)
OTHERS = tuple(b for b in range(27) if b != 13)


def groups_of():
    groups = []
    for k in (1, 2, 3):
        here = [b for b in OTHERS if NONZERO[b] == k and b < 13]
        per = ATOMS // (SLOTS * 2 // 2**k) // 2
        for first in range(0, len(here), per):
            some = here[first : first + per]
            groups.append(tuple(some) + tuple(26 - b for b in some))
    return tuple(groups)


GROUPS = groups_of()
NG = len(GROUPS)
BLOCKS = NG + 1
PLACE = {b: k for k, b in enumerate(OTHERS)}
GROUP = {b: g for g, some in enumerate(GROUPS) for b in some}
AT = {b: k * COUNT[b] for some in GROUPS for k, b in enumerate(some)}


def dot(a, b, ca, cb, precision=None):
    return lax.dot_general(
        a, b, (((ca,), (cb,)), ((), ())), preferred_element_type=F32, precision=precision
    )


def iota(shape, dim):
    return lax.broadcasted_iota(I32, shape, dim)


def hot(condition):
    return jnp.where(condition, 1.0, 0.0).astype(BF16)


def sigmoid(x):
    return 0.5 + 0.5 * jnp.tanh(0.5 * x)


def split(x):
    hi = x.astype(BF16)
    return hi, (x - hi.astype(F32)).astype(BF16)


def lanes(row, index):
    return jnp.take_along_axis(jnp.broadcast_to(row, index.shape), index, axis=1)


def kernel(
    sizes,
    feat_hbm,
    pos_hbm,
    wup_hbm,
    wbasis_hbm,
    whid_hbm,
    wrad_hbm,
    wmix_hbm,
    wread_hbm,
    wout_hbm,
    lists_hbm,
    send_hbm,
    slot_hbm,
    base_hbm,
    live_hbm,
    force_ref,
    energy_ref,
    feat_ref,
    pos_ref,
    wup_ref,
    wbasis_ref,
    whid_ref,
    wrad_ref,
    wmix_ref,
    wread_ref,
    wout_ref,
    lists_ref,
    send_ref,
    slot_ref,
    base_ref,
    live_ref,
    stage_sem,
    out_rows,
    out_xyz,
    table_b,
    in_xyz,
    table_t,
    table_c,
    chosen_ref,
    at_ref,
    h2_ref,
    rows_ref,
    g_ref,
    dr_ref,
    a_ref,
    d1_ref,
    d2_ref,
    p_ref,
    s_ref,
    u_ref,
    rad_ref,
    harm_ref,
    slots_ref,
    low_ref,
    high_ref,
    target_ref,
    dharm_ref,
    drad_ref,
    gsep_ref,
    acc_ref,
    racc_ref,
    out_grad,
    in_grad,
    wbt_ref,
    wht_ref,
    wrt_ref,
    wb3_ref,
    placel_ref,
    placer_ref,
    row_send,
    row_recv,
    xyz_send,
    xyz_recv,
    grad_send,
    grad_recv,
):
    here = tuple(lax.axis_index(name) for name in ("gx", "gy", "gz"))

    def device(b):
        return tuple(lax.rem(c + (d + n), n) for c, d, n in zip(here, DIRS[b], sizes))

    barrier = pltpu.get_barrier_semaphore()
    for b in OTHERS:
        pl.semaphore_signal(barrier, inc=1, device_id=device(b), device_id_type=MESH)

    staged = {}
    moves = (
        ("feat", feat_hbm, feat_ref),
        ("wup", wup_hbm, wup_ref),
        ("lists", lists_hbm, lists_ref),
        ("pos", pos_hbm, pos_ref),
        ("base", base_hbm, base_ref),
        ("live", live_hbm, live_ref),
        ("slot", slot_hbm, slot_ref),
        ("send", send_hbm, send_ref),
        ("wbasis", wbasis_hbm, wbasis_ref),
        ("whid", whid_hbm, whid_ref),
        ("wrad", wrad_hbm, wrad_ref),
        ("wmix", wmix_hbm, wmix_ref),
        ("wread", wread_hbm, wread_ref),
        ("wout", wout_hbm, wout_ref),
    )
    for k, (name, source, target) in enumerate(moves):
        staged[name] = pltpu.make_async_copy(source, target, stage_sem.at[k])
        staged[name].start()
    early = ("feat", "wup", "lists", "pos")
    for name in early:
        staged[name].wait()

    projected = dot(feat_ref[...], wup_ref[...], 1, 0).astype(BF16)
    table_b[0:ATOMS, :] = projected
    own = jnp.concatenate([pos_ref[d] for d in range(3)], axis=0)
    lane = iota((1, 128), 1)
    for g, some in enumerate(GROUPS):
        order = sorted(some, key=lambda b: AT[26 - b])
        named = jnp.concatenate([lists_ref[b][:, 0 : COUNT[b]] for b in order], axis=1)
        chosen = hot(iota((ATOMS, 128), 0) == named)
        chosen_ref[:, 128 * g : 128 * g + 128] = chosen
        out_rows[128 * g : 128 * g + 128, :] = dot(chosen, projected, 0, 0).astype(BF16)
        for d in range(3):
            shift = jnp.zeros((1, 128), F32)
            for b in some:
                if DIRS[b][d]:
                    inside = (lane >= AT[26 - b]) & (lane < AT[26 - b] + COUNT[b])
                    shift = jnp.where(inside, -SIDE * DIRS[b][d], shift)
            moved = lanes(own[d : d + 1, :], jnp.broadcast_to(named, (8, 128)))[0:1, :]
            out_xyz[g, d : d + 1, :] = moved + shift

    pl.semaphore_wait(barrier, 26)

    for b in OTHERS:
        pltpu.make_async_remote_copy(
            src_ref=out_xyz.at[GROUP[b]],
            dst_ref=in_xyz.at[PLACE[26 - b]],
            send_sem=xyz_send,
            recv_sem=xyz_recv,
            device_id=device(b),
            device_id_type=MESH,
        ).start()
    for b in OTHERS:
        n, g, spot = COUNT[b], GROUP[b], AT[26 - b]
        pltpu.make_async_remote_copy(
            src_ref=out_rows.at[pl.ds(128 * g + spot, n), :],
            dst_ref=table_b.at[pl.ds(128 * (g + 1) + spot, n), :],
            send_sem=row_send,
            recv_sem=row_recv,
            device_id=device(b),
            device_id_type=MESH,
        ).start()

    def wait_bytes(ref, sem):
        pltpu.make_async_copy(ref, ref, sem).wait()

    for name in staged:
        if name not in early:
            staged[name].wait()

    eye = hot(iota((128, 128), 0) == iota((128, 128), 1))
    eye64 = eye[0:64, 0:64]
    wb_hi, wb_lo = split(wbasis_ref[...])
    hi, lo = wb_hi.astype(F32), wb_lo.astype(F32)
    stacked = jnp.concatenate([hi, hi, lo, lo], axis=0).astype(BF16)
    wbt_ref[...] = dot(eye64, stacked, 1, 1).astype(BF16)
    wht_ref[...] = dot(eye64, whid_ref[...], 1, 1).astype(BF16)
    for degree in range(3):
        part = wrad_ref[:, degree * C : degree * C + C]
        wrt_ref[degree * C : degree * C + C, :] = dot(eye, part, 1, 1).astype(BF16)
    wb3_ref[...] = jnp.concatenate([hi, hi, lo], axis=1).astype(BF16)

    base_rows = jnp.broadcast_to(base_ref[...].astype(F32), (128, TILES)).astype(BF16)
    eye_tiles = hot(iota((TILES, TILES), 0) == iota((TILES, TILES), 1))
    base_tiles = dot(eye_tiles, base_rows, 1, 1)
    slots_ref[...] = jnp.where(iota((TILES, EDGE), 0) < live_ref[0, 0], slot_ref[...], RT)
    receiver = base_tiles.astype(I32) + jnp.minimum(slot_ref[...], RT - 1)
    target_ref[...] = receiver

    def place_lanes():
        reach = hot((iota((TILES, JR), 1) >> 3) == iota((TILES, JR), 0))
        expanded = dot(base_rows, reach, 1, 0).astype(I32) + (iota((128, JR), 1) & (RT - 1))
        return hot(expanded == iota((128, JR), 0))

    def place_rows():
        reach = hot((iota((JR, TILES), 0) >> 3) == iota((JR, TILES), 1))
        expanded = dot(reach, base_rows, 1, 1).astype(I32) + (iota((JR, 128), 0) & (RT - 1))
        return hot(expanded == iota((JR, 128), 1))

    placel_ref[...] = place_lanes()
    placer_ref[...] = place_rows()

    block_lane = iota((1, 128), 1)
    moved_by = jnp.zeros((1, 128), I32)
    for b in OTHERS:
        offset = 128 * (GROUP[b] + 1) + AT[b] - (ATOMS + b * SLOTS)
        moved_by = jnp.where(block_lane == b + 2, offset, moved_by)
    for g in range(TILES // 8):
        at = slice(8 * g, 8 * g + 8)
        entry = send_ref[at, :]
        entry = entry + lanes(moved_by, jnp.right_shift(entry, 6))
        low_ref[at, :] = jnp.bitwise_and(entry, 127)
        high_ref[at, :] = jnp.right_shift(entry, 7)

    wait_bytes(in_xyz, xyz_recv)
    wait_bytes(in_xyz, xyz_send)
    for d in range(3):
        table_c[0, d : d + 1, :] = own[d : d + 1, :]
    for g, some in enumerate(GROUPS):
        value = in_xyz[PLACE[some[0]], 0:3, :]
        for b in some[1:]:
            value = jnp.where(lane >= AT[b], in_xyz[PLACE[b], 0:3, :], value)
        table_c[g + 1, 0:3, :] = value

    for g in range(TILES // 8):
        at = slice(8 * g, 8 * g + 8)
        low, high = low_ref[at, :], high_ref[at, :]
        parts = []
        for d in range(3):
            value = lanes(table_c[0, d : d + 1, :], low)
            for k in range(1, BLOCKS):
                value = jnp.where(high == k, lanes(table_c[k, d : d + 1, :], low), value)
            u = (value - lanes(own[d : d + 1, :], receiver[at, :])) * INV_CUT
            u_ref[d, at, :] = u
            parts.append(u)
        ux, uy, uz = parts
        xx, yy, zz = ux * ux, uy * uy, uz * uz
        rad_ref[at, :] = xx + yy + zz
        values = (
            R3 * ux,
            R3 * uy,
            R3 * uz,
            R15 * ux * uy,
            R15 * uy * uz,
            0.5 * R5 * (2.0 * zz - xx - yy),
            R15 * ux * uz,
            0.5 * R15 * (xx - yy),
        )
        for m, value in enumerate(values):
            harm_ref[m, at, :] = value

    decay = (iota((NB, PE), 0).astype(F32) + 1.0) * 0.5
    slot_ids = iota((RP, PE), 0)
    half_shift = jnp.where(iota((1, PE), 1) < EDGE, 0, RT)
    row_ids = iota((128, PE), 0).astype(F32).astype(BF16)
    inner = range(PER_STEP)

    def tiles_of(ref, first, count):
        return jnp.concatenate([ref[pl.ds(first + k, 1), :] for k in range(count)], axis=1)

    def onehot_of(first):
        pair = tiles_of(slots_ref, first, 2)
        pair = jnp.where(pair < RT, pair + half_shift, RP)
        return jnp.where(slot_ids == pair, 1.0, 0.0)

    def radial_parts(pair):
        s = tiles_of(rad_ref, 2 * pair, 2)
        reach = jnp.maximum(1.0 - s * s, 0.0)
        return s, reach, jnp.exp(-decay * s)

    def gather(pair):
        low = tiles_of(low_ref, 2 * pair, 2)
        high = tiles_of(high_ref, 2 * pair, 2)
        at_low = jnp.where(row_ids == low.astype(F32).astype(BF16), jnp.ones((), BF16), jnp.zeros((), BF16))
        at_ref[pair] = at_low
        entries = jnp.concatenate([at_low * hot(high == k) for k in range(BLOCKS)], axis=0)
        rows_ref[pair] = dot(table_t[...], entries, 1, 0).astype(BF16)

    def network(step, carry):
        pairs = [step * NETWORK + q for q in range(NETWORK)]
        basis4 = []
        for pair in pairs:
            s, reach, fall = radial_parts(pair)
            basis = fall * (reach * reach)
            hi = basis.astype(BF16).astype(F32)
            lo = basis - hi
            basis4.append(jnp.concatenate([hi, lo, hi, lo], axis=0).astype(BF16))
        pre1 = [dot(wbt_ref[...], value, 1, 0) for value in basis4]
        act1 = []
        for pair, pre in zip(pairs, pre1):
            sig = sigmoid(pre)
            act = pre * sig
            d1_ref[pair] = sig + act * (1.0 - sig)
            act1.append(act.astype(BF16))
        pre2 = [dot(wht_ref[...], value, 1, 0) for value in act1]
        for pair, pre in zip(pairs, pre2):
            sig = sigmoid(pre)
            act = pre * sig
            d2_ref[pair] = sig + act * (1.0 - sig)
            h2_ref[pair] = act.astype(BF16)
        return carry

    lax.fori_loop(0, TILES // 2 // NETWORK, network, 0)

    wait_bytes(table_b.at[pl.ds(ATOMS, NG * 128), :], row_recv)
    wait_bytes(out_rows, row_send)
    for k in range(BLOCKS):
        block = table_b[128 * k : 128 * k + 128, :]
        table_t[:, 128 * k : 128 * k + 128] = dot(eye, block, 1, 1).astype(BF16)

    def gathered(step):
        for q in inner:
            pair = step * PER_STEP + q
            onehot = onehot_of(2 * pair)
            weights = [onehot]
            for m in range(8):
                weights.append(onehot * tiles_of(harm_ref.at[m], 2 * pair, 2))
            weights = jnp.concatenate(weights, axis=0).astype(BF16)
            a_ref[pair] = weights
            rows = rows_ref[pair]
            place = pl.ds(pair * RP, RP)
            radial = dot(wrt_ref[...], h2_ref[pair], 1, 0).astype(BF16)
            for degree, (first, last) in enumerate(SPANS):
                across = slice(degree * C, degree * C + C)
                g = radial[across, :] * rows
                g_ref[pair, across, :] = g
                part = dot(weights[first * RP : last * RP, :], g, 1, 1).astype(BF16)
                for m in range(first, last):
                    p_ref[place, m * C : m * C + C] = part[
                        (m - first) * RP : (m - first) * RP + RP, :
                    ]

    def forward(step, carry):
        gathered(lax.rem(step + (STEPS - 1), STEPS))
        for q in inner:
            gather(step * PER_STEP + q)
        return carry

    lax.fori_loop(0, STEPS, forward, 0)
    gathered(STEPS - 1)

    sums = dot(placel_ref[...], p_ref[...], 1, 0)
    halves = [0.5 * sums[:, m * C : m * C + C] for m in range(9)]
    inv = [halves[0]]
    for first, last in SPANS[1:]:
        total = halves[first] * halves[first]
        for m in range(first + 1, last):
            total = total + halves[m] * halves[m]
        inv.append(total)
    invariants = jnp.concatenate(inv, axis=1).astype(BF16)
    updated = feat_ref[...].astype(F32) + dot(invariants, wmix_ref[...], 1, 0)
    high = lax.Precision.HIGHEST
    pre = dot(wread_ref[...], updated, 1, 1, high)
    sig = sigmoid(pre)
    act = pre * sig
    row = iota((RO, ATOMS), 0)
    outw = jnp.zeros((RO, ATOMS), F32)
    for r in range(RO):
        outw = jnp.where(row == r, wout_ref[r], outw)
    energy_ref[...] = jnp.sum(outw * act, axis=0, keepdims=True)
    dpre = outw * (sig + act * (1.0 - sig))
    dupd = dot(dpre, wread_ref[...], 0, 0, high)
    dinv = dot(dupd.astype(BF16), wmix_ref[...], 1, 1).astype(BF16).astype(F32)
    grads = []
    for m in range(9):
        part = dinv[:, DEGREE[m] * C : DEGREE[m] * C + C]
        grads.append(0.5 * part if m == 0 else halves[m] * part)
    grads = jnp.concatenate(grads, axis=1).astype(BF16)
    s_ref[...] = dot(placer_ref[...], grads, 1, 0).astype(BF16)

    acc_ref[...] = jnp.zeros_like(acc_ref)
    racc_ref[...] = jnp.zeros_like(racc_ref)

    def to_edges(step):
        for q in inner:
            pair = step * PER_STEP + q
            onehot = onehot_of(2 * pair)
            place = pl.ds(pair * RP, RP)
            rows = rows_ref[pair]
            for degree, (first, last) in enumerate(SPANS):
                cot = jnp.concatenate(
                    [s_ref[place, m * C : m * C + C] for m in range(first, last)], axis=0
                )
                across = slice(degree * C, degree * C + C)
                dg = dot(cot, a_ref[pair, first * RP : last * RP, :], 0, 0)
                dr_ref[pair, across, :] = dg.astype(BF16) * rows
                if degree:
                    back = dot(cot, g_ref[pair, across, :], 1, 0)
                    for m in range(first, last):
                        one = back[(m - first) * RP : (m - first) * RP + RP, :]
                        dh = jnp.sum(one * onehot, axis=0, keepdims=True)
                        dharm_ref[m, pl.ds(2 * pair, 1), :] = dh[:, 0:EDGE]
                        dharm_ref[m, pl.ds(2 * pair + 1, 1), :] = dh[:, EDGE:PE]

    def to_radius(step):
        pairs = [step * PER_STEP + q for q in inner]
        dact2 = [dot(wrad_ref[...], dr_ref[pair], 1, 0) for pair in pairs]
        dpre2 = [(value * d2_ref[pair]).astype(BF16) for value, pair in zip(dact2, pairs)]
        dact1 = [dot(whid_ref[...], value, 1, 0) for value in dpre2]
        stacks = []
        for value, pair in zip(dact1, pairs):
            hi, lo = split(value * d1_ref[pair])
            stacks.append(jnp.concatenate([hi, lo, hi], axis=0))
        dbasis = [dot(wb3_ref[...], value, 1, 0) for value in stacks]
        for value, pair in zip(dbasis, pairs):
            s, reach, fall = radial_parts(pair)
            slope = fall * (-decay * (reach * reach) - (4.0 * s) * reach)
            ds = jnp.sum(value * slope, axis=0, keepdims=True)
            drad_ref[pl.ds(2 * pair, 1), :] = ds[:, 0:EDGE]
            drad_ref[pl.ds(2 * pair + 1, 1), :] = ds[:, EDGE:PE]

    def scatter(step, counts):
        at = pl.ds(pl.multiple_of(step * TS, TS), TS)
        ux, uy, uz = u_ref[0, at, :], u_ref[1, at, :], u_ref[2, at, :]
        twice = 2.0 * drad_ref[at, :]
        dh = [None] + [dharm_ref[m, at, :] for m in range(1, 9)]
        gx = R3 * dh[1] + R15 * (uy * dh[4] + uz * dh[7] + ux * dh[8]) - R5 * (ux * dh[6])
        gy = R3 * dh[2] + R15 * (ux * dh[4] + uz * dh[5] - uy * dh[8]) - R5 * (uy * dh[6])
        gz = R3 * dh[3] + R15 * (uy * dh[5] + ux * dh[7]) + (2.0 * R5) * (uz * dh[6])
        for d, value in enumerate((twice * ux + gx, twice * uy + gy, twice * uz + gz)):
            g = jnp.where(counts, value * INV_CUT, 0.0)
            hi = g.astype(BF16).astype(F32)
            gsep_ref[2 * d] = hi
            gsep_ref[2 * d + 1] = g - hi
        at_high = iota((8, ES), 0) == tiles_of(high_ref, step * TS, TS)
        at_target = hot(iota((128, ES), 0) == tiles_of(target_ref, step * TS, TS))
        at_low = jnp.concatenate([at_ref[step * PER_STEP + q] for q in inner], axis=1)
        row8 = iota((8, ES), 0)
        left, stack = [], jnp.zeros((8, ES), F32)
        for k in range(6):
            value = tiles_of(gsep_ref.at[k], 0, TS)
            left.append(jnp.where(at_high, value, 0.0))
            stack = jnp.where(row8 == k, value, stack)
        acc_ref[...] += dot(jnp.concatenate(left, axis=0).astype(BF16), at_low, 1, 1)
        racc_ref[...] += dot(stack.astype(BF16), at_target, 1, 1)

    def backward(step, carry):
        scatter(lax.rem(step + (STEPS - 2), STEPS), step >= 2)
        to_radius(lax.rem(step + (STEPS - 1), STEPS))
        to_edges(step)
        return carry

    lax.fori_loop(0, STEPS, backward, 0)
    scatter(STEPS - 2, True)
    to_radius(STEPS - 1)
    scatter(STEPS - 1, True)

    for d in range(3):
        grid = acc_ref[16 * d : 16 * d + 8, :] + acc_ref[16 * d + 8 : 16 * d + 16, :]
        for g in range(NG):
            out_grad[g, d : d + 1, :] = grid[g + 1 : g + 2, :]
        mine = racc_ref[2 * d : 2 * d + 1, :] + racc_ref[2 * d + 1 : 2 * d + 2, :]
        force_ref[d] = mine - grid[0:1, :]

    for b in OTHERS:
        pltpu.make_async_remote_copy(
            src_ref=out_grad.at[GROUP[b]],
            dst_ref=in_grad.at[PLACE[26 - b]],
            send_sem=grad_send,
            recv_sem=grad_recv,
            device_id=device(b),
            device_id_type=MESH,
        ).start()
    wait_bytes(in_grad, grad_recv)
    wait_bytes(in_grad, grad_send)

    stacks = []
    for some in GROUPS:
        order = sorted(some, key=lambda b: AT[26 - b])
        came = in_grad[PLACE[order[0]], 0:3, :]
        for b in order[1:]:
            came = jnp.where(lane >= AT[26 - b], in_grad[PLACE[b], 0:3, :], came)
        hi = came.astype(BF16).astype(F32)
        stacks.append(jnp.concatenate([hi, came - hi], axis=0))
    stacks = jnp.concatenate(stacks, axis=1).astype(BF16)
    total = dot(stacks, chosen_ref[...], 1, 1)
    for d in range(3):
        force_ref[d] = force_ref[d] - (total[d : d + 1, :] + total[d + 3 : d + 4, :])


def solution(mesh):
    sizes = tuple(mesh.shape[name] for name in ("gx", "gy", "gz"))
    vmem = pl.BlockSpec(memory_space=pltpu.VMEM)
    hbm = pl.BlockSpec(memory_space=pltpu.HBM)
    pairs = TILES // 2

    def step(
        features,
        positions,
        w_up,
        w_basis,
        w_hidden,
        w_radial,
        w_mix,
        w_read,
        w_out,
        send_lists,
        tile_senders,
        tile_slots,
        tile_bases,
        tile_live,
    ):
        dma = pltpu.SemaphoreType.DMA
        force, energy = pl.pallas_call(
            functools.partial(kernel, sizes),
            out_shape=(
                jax.ShapeDtypeStruct((3, 1, ATOMS), F32),
                jax.ShapeDtypeStruct((1, ATOMS), F32),
            ),
            in_specs=[hbm] * 14,
            out_specs=(vmem, vmem),
            scratch_shapes=[
                pltpu.VMEM((ATOMS, C), BF16),
                pltpu.VMEM((3, 1, ATOMS), F32),
                pltpu.VMEM((C, C), BF16),
                pltpu.VMEM((NB, RH), F32),
                pltpu.VMEM((RH, RH), BF16),
                pltpu.VMEM((RH, 3 * C), BF16),
                pltpu.VMEM((3 * C, C), BF16),
                pltpu.VMEM((RO, C), F32),
                pltpu.SMEM((RO,), F32),
                pltpu.VMEM((27, 1, SLOTS), I32),
                pltpu.VMEM((TILES, EDGE), I32),
                pltpu.VMEM((TILES, EDGE), I32),
                pltpu.VMEM((1, TILES), I32),
                pltpu.SMEM((1, 1), I32),
                pltpu.SemaphoreType.DMA((14,)),
                pltpu.VMEM((NG * 128, C), BF16),
                pltpu.VMEM((NG, 4, 128), F32),
                pltpu.VMEM((BLOCKS * 128, C), BF16),
                pltpu.VMEM((26, 4, 128), F32),
                pltpu.VMEM((C, BLOCKS * 128), BF16),
                pltpu.VMEM((BLOCKS, 8, 128), F32),
                pltpu.VMEM((ATOMS, NG * 128), BF16),
                pltpu.VMEM((pairs, 128, PE), BF16),
                pltpu.VMEM((pairs, RH, PE), BF16),
                pltpu.VMEM((pairs, C, PE), BF16),
                pltpu.VMEM((pairs, 3 * C, PE), BF16),
                pltpu.VMEM((pairs, 3 * C, PE), BF16),
                pltpu.VMEM((pairs, 9 * RP, PE), BF16),
                pltpu.VMEM((pairs, RH, PE), F32),
                pltpu.VMEM((pairs, RH, PE), F32),
                pltpu.VMEM((JR, 9 * C), BF16),
                pltpu.VMEM((JR, 9 * C), BF16),
                pltpu.VMEM((3, TILES, EDGE), F32),
                pltpu.VMEM((TILES, EDGE), F32),
                pltpu.VMEM((8, TILES, EDGE), F32),
                pltpu.VMEM((TILES, EDGE), I32),
                pltpu.VMEM((TILES, EDGE), I32),
                pltpu.VMEM((TILES, EDGE), I32),
                pltpu.VMEM((TILES, EDGE), I32),
                pltpu.VMEM((9, TILES, EDGE), F32),
                pltpu.VMEM((TILES, EDGE), F32),
                pltpu.VMEM((6, TS, EDGE), F32),
                pltpu.VMEM((48, 128), F32),
                pltpu.VMEM((8, 128), F32),
                pltpu.VMEM((NG, 4, 128), F32),
                pltpu.VMEM((26, 4, 128), F32),
                pltpu.VMEM((RH, 4 * NB), BF16),
                pltpu.VMEM((RH, RH), BF16),
                pltpu.VMEM((3 * C, RH), BF16),
                pltpu.VMEM((NB, 3 * RH), BF16),
                pltpu.VMEM((ATOMS, JR), BF16),
                pltpu.VMEM((JR, ATOMS), BF16),
                dma,
                dma,
                dma,
                dma,
                dma,
                dma,
            ],
            compiler_params=pltpu.CompilerParams(
                collective_id=0,
                has_side_effects=True,
                vmem_limit_bytes=64 * 2**20 - 65536,
            ),
        )(
            features.reshape(ATOMS, C),
            positions.reshape(3, 1, ATOMS),
            w_up,
            w_basis,
            w_hidden,
            w_radial,
            w_mix,
            w_read.T,
            w_out,
            send_lists.reshape(27, 1, SLOTS),
            tile_senders.reshape(TILES, EDGE),
            tile_slots.reshape(TILES, EDGE),
            tile_bases.reshape(1, TILES),
            tile_live.reshape(1, 1),
        )
        return force.reshape(1, 1, 1, 3, ATOMS), energy.reshape(1, 1, 1, ATOMS)

    cube = ("gx", "gy", "gz")
    return jax.shard_map(
        step,
        mesh=mesh,
        in_specs=(
            P(*cube, None, None),
            P(*cube, None, None),
            P(),
            P(),
            P(),
            P(),
            P(),
            P(),
            P(),
            P(*cube, None, None, None, None),
            P(*cube, None, None),
            P(*cube, None, None),
            P(*cube, None),
            P(*cube),
        ),
        out_specs=(P(*cube, None, None), P(*cube, None)),
        check_vma=False,
    )
```

```python
import functools

import jax
import jax.numpy as jnp
from jax import lax
from jax.experimental import pallas as pl
from jax.experimental.pallas import tpu as pltpu
from jax.sharding import PartitionSpec as P

MESH = pl.DeviceIdType.MESH
F32 = jnp.float32
BF16 = jnp.bfloat16
I32 = jnp.int32

ATOMS = 128
C = 128
SLOTS = 64
TILES = 64
EDGE = 128
RT = 8
RH = 64
NB = 8
RO = 16
JR = TILES * RT
PE = 2 * EDGE
RP = 2 * RT
PER_STEP = 4
STEPS = TILES // 2 // PER_STEP
ES = PE * PER_STEP
NETWORK = 8
TS = 2 * PER_STEP

SIDE = 11.0
INV_CUT = 0.2
R3 = 3.0**0.5
R5 = 5.0**0.5
R15 = 15.0**0.5
DEGREE = (0, 1, 1, 1, 2, 2, 2, 2, 2)
SPANS = ((0, 1), (1, 4), (4, 9))

DIRS = tuple((b // 9 - 1, b // 3 % 3 - 1, b % 3 - 1) for b in range(27))
NONZERO = tuple(sum(v != 0 for v in d) for d in DIRS)
COUNT = tuple(SLOTS * 2 // 2 ** max(k, 1) for k in NONZERO)
OTHERS = tuple(b for b in range(27) if b != 13)


def groups_of():
    groups = []
    for k in (1, 2, 3):
        here = [b for b in OTHERS if NONZERO[b] == k and b < 13]
        per = ATOMS // (SLOTS * 2 // 2**k) // 2
        for first in range(0, len(here), per):
            some = here[first : first + per]
            groups.append(tuple(some) + tuple(26 - b for b in some))
    return tuple(groups)


GROUPS = groups_of()
NG = len(GROUPS)
BLOCKS = NG + 1
PLACE = {b: k for k, b in enumerate(OTHERS)}
GROUP = {b: g for g, some in enumerate(GROUPS) for b in some}
AT = {b: k * COUNT[b] for some in GROUPS for k, b in enumerate(some)}


def dot(a, b, ca, cb, precision=None):
    return lax.dot_general(
        a, b, (((ca,), (cb,)), ((), ())), preferred_element_type=F32, precision=precision
    )


def iota(shape, dim):
    return lax.broadcasted_iota(I32, shape, dim)


def hot(condition):
    return jnp.where(condition, 1.0, 0.0).astype(BF16)


def sigmoid(x):
    return 0.5 + 0.5 * jnp.tanh(0.5 * x)


def split(x):
    hi = x.astype(BF16)
    return hi, (x - hi.astype(F32)).astype(BF16)


def lanes(row, index):
    return jnp.take_along_axis(jnp.broadcast_to(row, index.shape), index, axis=1)


def kernel(
    sizes,
    feat_hbm,
    pos_hbm,
    wup_hbm,
    wbasis_hbm,
    whid_hbm,
    wrad_hbm,
    wmix_hbm,
    wread_hbm,
    wout_hbm,
    lists_hbm,
    send_hbm,
    slot_hbm,
    base_hbm,
    live_hbm,
    force_ref,
    feat_ref,
    pos_ref,
    wup_ref,
    wbasis_ref,
    whid_ref,
    wrad_ref,
    wmix_ref,
    wread_ref,
    wout_ref,
    lists_ref,
    send_ref,
    slot_ref,
    base_ref,
    live_ref,
    stage_sem,
    out_rows,
    out_xyz,
    table_b,
    in_xyz,
    table_t,
    table_c,
    chosen_ref,
    at_ref,
    h2_ref,
    rows_ref,
    g_ref,
    dr_ref,
    a_ref,
    d1_ref,
    d2_ref,
    p_ref,
    s_ref,
    u_ref,
    rad_ref,
    harm_ref,
    slots_ref,
    low_ref,
    high_ref,
    target_ref,
    dharm_ref,
    drad_ref,
    gsep_ref,
    acc_ref,
    racc_ref,
    out_grad,
    in_grad,
    wbt_ref,
    wht_ref,
    wrt_ref,
    wb3_ref,
    placel_ref,
    placer_ref,
    row_send,
    row_recv,
    xyz_send,
    xyz_recv,
    grad_send,
    grad_recv,
):
    here = tuple(lax.axis_index(name) for name in ("gx", "gy", "gz"))

    def device(b):
        return tuple(lax.rem(c + (d + n), n) for c, d, n in zip(here, DIRS[b], sizes))

    staged = {}
    moves = (
        ("lists", lists_hbm, lists_ref),
        ("pos", pos_hbm, pos_ref),
        ("feat", feat_hbm, feat_ref),
        ("wup", wup_hbm, wup_ref),
        ("base", base_hbm, base_ref),
        ("live", live_hbm, live_ref),
        ("slot", slot_hbm, slot_ref),
        ("send", send_hbm, send_ref),
        ("wbasis", wbasis_hbm, wbasis_ref),
        ("whid", whid_hbm, whid_ref),
        ("wrad", wrad_hbm, wrad_ref),
        ("wmix", wmix_hbm, wmix_ref),
        ("wread", wread_hbm, wread_ref),
        ("wout", wout_hbm, wout_ref),
    )
    early = ("lists", "pos", "feat", "wup")
    for k, (name, source, target) in enumerate(moves):
        staged[name] = pltpu.make_async_copy(source, target, stage_sem.at[k])
        if name in early:
            staged[name].start()
    barrier = pltpu.get_barrier_semaphore()
    for b in OTHERS:
        pl.semaphore_signal(barrier, inc=1, device_id=device(b), device_id_type=MESH)
    for name in staged:
        if name not in early:
            staged[name].start()

    staged["lists"].wait()
    staged["pos"].wait()
    own = jnp.concatenate([pos_ref[d] for d in range(3)], axis=0)
    lane = iota((1, 128), 1)
    for g, some in enumerate(GROUPS):
        order = sorted(some, key=lambda b: AT[26 - b])
        named = jnp.concatenate([lists_ref[b][:, 0 : COUNT[b]] for b in order], axis=1)
        chosen_ref[:, 128 * g : 128 * g + 128] = hot(iota((ATOMS, 128), 0) == named)
        for d in range(3):
            shift = jnp.zeros((1, 128), F32)
            for b in some:
                if DIRS[b][d]:
                    inside = (lane >= AT[26 - b]) & (lane < AT[26 - b] + COUNT[b])
                    shift = jnp.where(inside, -SIDE * DIRS[b][d], shift)
            moved = lanes(own[d : d + 1, :], jnp.broadcast_to(named, (8, 128)))[0:1, :]
            out_xyz[g, d : d + 1, :] = moved + shift

    pl.semaphore_wait(barrier, 26)

    for b in OTHERS:
        pltpu.make_async_remote_copy(
            src_ref=out_xyz.at[GROUP[b]],
            dst_ref=in_xyz.at[PLACE[26 - b]],
            send_sem=xyz_send,
            recv_sem=xyz_recv,
            device_id=device(b),
            device_id_type=MESH,
        ).start()
    staged["feat"].wait()
    staged["wup"].wait()
    projected = dot(feat_ref[...], wup_ref[...], 1, 0).astype(BF16)
    table_b[0:ATOMS, :] = projected
    for g in range(NG):
        at = slice(128 * g, 128 * g + 128)
        out_rows[at, :] = dot(chosen_ref[:, at], projected, 0, 0).astype(BF16)
    for b in OTHERS:
        n, g, spot = COUNT[b], GROUP[b], AT[26 - b]
        pltpu.make_async_remote_copy(
            src_ref=out_rows.at[pl.ds(128 * g + spot, n), :],
            dst_ref=table_b.at[pl.ds(128 * (g + 1) + spot, n), :],
            send_sem=row_send,
            recv_sem=row_recv,
            device_id=device(b),
            device_id_type=MESH,
        ).start()

    def wait_bytes(ref, sem):
        pltpu.make_async_copy(ref, ref, sem).wait()

    for name in staged:
        if name not in early:
            staged[name].wait()

    eye = hot(iota((128, 128), 0) == iota((128, 128), 1))
    eye64 = eye[0:64, 0:64]
    wb_hi, wb_lo = split(wbasis_ref[...])
    hi, lo = wb_hi.astype(F32), wb_lo.astype(F32)
    stacked = jnp.concatenate([hi, hi, lo, lo], axis=0).astype(BF16)
    wbt_ref[...] = dot(eye64, stacked, 1, 1).astype(BF16)
    wht_ref[...] = dot(eye64, whid_ref[...], 1, 1).astype(BF16)
    for degree in range(3):
        part = wrad_ref[:, degree * C : degree * C + C]
        wrt_ref[degree * C : degree * C + C, :] = dot(eye, part, 1, 1).astype(BF16)
    wb3_ref[...] = jnp.concatenate([hi, lo], axis=0).astype(BF16)

    base_rows = jnp.broadcast_to(base_ref[...].astype(F32), (128, TILES)).astype(BF16)
    eye_tiles = hot(iota((TILES, TILES), 0) == iota((TILES, TILES), 1))
    base_tiles = dot(eye_tiles, base_rows, 1, 1)
    slots_ref[...] = jnp.where(iota((TILES, EDGE), 0) < live_ref[0, 0], slot_ref[...], RT)
    receiver = base_tiles.astype(I32) + jnp.minimum(slot_ref[...], RT - 1)
    target_ref[...] = receiver

    def place_lanes():
        reach = hot((iota((TILES, JR), 1) >> 3) == iota((TILES, JR), 0))
        expanded = dot(base_rows, reach, 1, 0).astype(I32) + (iota((128, JR), 1) & (RT - 1))
        return hot(expanded == iota((128, JR), 0))

    def place_rows():
        reach = hot((iota((JR, TILES), 0) >> 3) == iota((JR, TILES), 1))
        expanded = dot(reach, base_rows, 1, 1).astype(I32) + (iota((JR, 128), 0) & (RT - 1))
        return hot(expanded == iota((JR, 128), 1))

    placel_ref[...] = place_lanes()
    placer_ref[...] = place_rows()

    block_lane = iota((1, 128), 1)
    moved_by = jnp.zeros((1, 128), I32)
    for b in OTHERS:
        offset = 128 * (GROUP[b] + 1) + AT[b] - (ATOMS + b * SLOTS)
        moved_by = jnp.where(block_lane == b + 2, offset, moved_by)
    for g in range(TILES // 8):
        at = slice(8 * g, 8 * g + 8)
        entry = send_ref[at, :]
        entry = entry + lanes(moved_by, jnp.right_shift(entry, 6))
        low_ref[at, :] = jnp.bitwise_and(entry, 127)
        high_ref[at, :] = jnp.right_shift(entry, 7)

    wait_bytes(in_xyz, xyz_recv)
    wait_bytes(in_xyz, xyz_send)
    for d in range(3):
        table_c[0, d : d + 1, :] = own[d : d + 1, :]
    for g, some in enumerate(GROUPS):
        value = in_xyz[PLACE[some[0]], 0:3, :]
        for b in some[1:]:
            value = jnp.where(lane >= AT[b], in_xyz[PLACE[b], 0:3, :], value)
        table_c[g + 1, 0:3, :] = value

    for g in range(TILES // 8):
        at = slice(8 * g, 8 * g + 8)
        low, high = low_ref[at, :], high_ref[at, :]
        parts = []
        for d in range(3):
            value = lanes(table_c[0, d : d + 1, :], low)
            for k in range(1, BLOCKS):
                value = jnp.where(high == k, lanes(table_c[k, d : d + 1, :], low), value)
            u = (value - lanes(own[d : d + 1, :], receiver[at, :])) * INV_CUT
            u_ref[d, at, :] = u
            parts.append(u)
        ux, uy, uz = parts
        xx, yy, zz = ux * ux, uy * uy, uz * uz
        rad_ref[at, :] = xx + yy + zz
        values = (
            R3 * ux,
            R3 * uy,
            R3 * uz,
            R15 * ux * uy,
            R15 * uy * uz,
            0.5 * R5 * (2.0 * zz - xx - yy),
            R15 * ux * uz,
            0.5 * R15 * (xx - yy),
        )
        for m, value in enumerate(values):
            harm_ref[m, at, :] = value

    decay = (iota((NB, PE), 0).astype(F32) + 1.0) * 0.5
    slot_ids = iota((RP, PE), 0)
    half_shift = jnp.where(iota((1, PE), 1) < EDGE, 0, RT)
    row_ids = iota((128, PE), 0).astype(F32).astype(BF16)
    inner = range(PER_STEP)

    def tiles_of(ref, first, count):
        return jnp.concatenate([ref[pl.ds(first + k, 1), :] for k in range(count)], axis=1)

    def onehot_of(first):
        pair = tiles_of(slots_ref, first, 2)
        pair = jnp.where(pair < RT, pair + half_shift, RP)
        return jnp.where(slot_ids == pair, 1.0, 0.0)

    def radial_parts(pair):
        s = tiles_of(rad_ref, 2 * pair, 2)
        reach = jnp.maximum(1.0 - s * s, 0.0)
        return s, reach, jnp.exp(-decay * s)

    def gather(pair):
        low = tiles_of(low_ref, 2 * pair, 2)
        high = tiles_of(high_ref, 2 * pair, 2)
        at_low = jnp.where(row_ids == low.astype(F32).astype(BF16), jnp.ones((), BF16), jnp.zeros((), BF16))
        at_ref[pair] = at_low
        entries = jnp.concatenate([at_low * hot(high == k) for k in range(BLOCKS)], axis=0)
        rows_ref[pair] = dot(table_t[...], entries, 1, 0).astype(BF16)

    def network(step, carry):
        pairs = [step * NETWORK + q for q in range(NETWORK)]
        basis4 = []
        for pair in pairs:
            s, reach, fall = radial_parts(pair)
            basis = fall * (reach * reach)
            hi = basis.astype(BF16).astype(F32)
            lo = basis - hi
            basis4.append(jnp.concatenate([hi, lo, hi, lo], axis=0).astype(BF16))
        pre1 = [dot(wbt_ref[...], value, 1, 0) for value in basis4]
        act1 = []
        for pair, pre in zip(pairs, pre1):
            sig = sigmoid(pre)
            act = pre * sig
            d1_ref[pair] = sig + act * (1.0 - sig)
            act1.append(act.astype(BF16))
        pre2 = [dot(wht_ref[...], value, 1, 0) for value in act1]
        for pair, pre in zip(pairs, pre2):
            sig = sigmoid(pre)
            act = pre * sig
            d2_ref[pair] = sig + act * (1.0 - sig)
            h2_ref[pair] = act.astype(BF16)
        return carry

    lax.fori_loop(0, TILES // 2 // NETWORK, network, 0)

    wait_bytes(table_b.at[pl.ds(ATOMS, NG * 128), :], row_recv)
    wait_bytes(out_rows, row_send)
    for k in range(BLOCKS):
        block = table_b[128 * k : 128 * k + 128, :]
        table_t[:, 128 * k : 128 * k + 128] = dot(eye, block, 1, 1).astype(BF16)

    def gathered(step):
        for q in inner:
            pair = step * PER_STEP + q
            onehot = onehot_of(2 * pair)
            weights = [onehot]
            for m in range(8):
                weights.append(onehot * tiles_of(harm_ref.at[m], 2 * pair, 2))
            weights = jnp.concatenate(weights, axis=0).astype(BF16)
            a_ref[pair] = weights
            rows = rows_ref[pair]
            place = pl.ds(pair * RP, RP)
            radial = dot(wrt_ref[...], h2_ref[pair], 1, 0).astype(BF16)
            for degree, (first, last) in enumerate(SPANS):
                across = slice(degree * C, degree * C + C)
                g = radial[across, :] * rows
                g_ref[pair, across, :] = g
                part = dot(weights[first * RP : last * RP, :], g, 1, 1).astype(BF16)
                for m in range(first, last):
                    p_ref[place, m * C : m * C + C] = part[
                        (m - first) * RP : (m - first) * RP + RP, :
                    ]

    def forward(step, carry):
        gathered(lax.rem(step + (STEPS - 1), STEPS))
        for q in inner:
            gather(step * PER_STEP + q)
        return carry

    lax.fori_loop(0, STEPS, forward, 0)
    gathered(STEPS - 1)

    sums = dot(placel_ref[...], p_ref[...], 1, 0)
    halves = [0.5 * sums[:, m * C : m * C + C] for m in range(9)]
    inv = [halves[0]]
    for first, last in SPANS[1:]:
        total = halves[first] * halves[first]
        for m in range(first + 1, last):
            total = total + halves[m] * halves[m]
        inv.append(total)
    invariants = jnp.concatenate(inv, axis=1).astype(BF16)
    updated = feat_ref[...].astype(F32) + dot(invariants, wmix_ref[...], 1, 0)
    high = lax.Precision.HIGHEST
    pre = dot(wread_ref[...], updated, 1, 1, high)
    sig = sigmoid(pre)
    act = pre * sig
    row = iota((RO, ATOMS), 0)
    outw = jnp.zeros((RO, ATOMS), F32)
    for r in range(RO):
        outw = jnp.where(row == r, wout_ref[r], outw)
    force_ref[3] = jnp.sum(outw * act, axis=0, keepdims=True)
    dpre = outw * (sig + act * (1.0 - sig))
    dupd = dot(dpre, wread_ref[...], 0, 0, high)
    dinv = dot(dupd.astype(BF16), wmix_ref[...], 1, 1).astype(BF16).astype(F32)
    grads = []
    for m in range(9):
        part = dinv[:, DEGREE[m] * C : DEGREE[m] * C + C]
        grads.append(0.5 * part if m == 0 else halves[m] * part)
    grads = jnp.concatenate(grads, axis=1).astype(BF16)
    s_ref[...] = dot(placer_ref[...], grads, 1, 0).astype(BF16)

    acc_ref[...] = jnp.zeros_like(acc_ref)
    racc_ref[...] = jnp.zeros_like(racc_ref)

    def to_edges(step):
        for q in inner:
            pair = step * PER_STEP + q
            onehot = onehot_of(2 * pair)
            place = pl.ds(pair * RP, RP)
            rows = rows_ref[pair]
            for degree, (first, last) in enumerate(SPANS):
                cot = jnp.concatenate(
                    [s_ref[place, m * C : m * C + C] for m in range(first, last)], axis=0
                )
                across = slice(degree * C, degree * C + C)
                dg = dot(cot, a_ref[pair, first * RP : last * RP, :], 0, 0)
                dr_ref[pair, across, :] = dg.astype(BF16) * rows
                if degree:
                    back = dot(cot, g_ref[pair, across, :], 1, 0)
                    for m in range(first, last):
                        one = back[(m - first) * RP : (m - first) * RP + RP, :]
                        dh = jnp.sum(one * onehot, axis=0, keepdims=True)
                        dharm_ref[m, pl.ds(2 * pair, 1), :] = dh[:, 0:EDGE]
                        dharm_ref[m, pl.ds(2 * pair + 1, 1), :] = dh[:, EDGE:PE]

    def to_radius(step):
        pairs = [step * PER_STEP + q for q in inner]
        dact2 = [dot(wrad_ref[...], dr_ref[pair], 1, 0) for pair in pairs]
        dpre2 = [(value * d2_ref[pair]).astype(BF16) for value, pair in zip(dact2, pairs)]
        dact1 = [dot(whid_ref[...], value, 1, 0) for value in dpre2]
        stacks = []
        for value, pair in zip(dact1, pairs):
            stacks.append((value * d1_ref[pair]).astype(BF16))
        dbasis = [dot(wb3_ref[...], value, 1, 0) for value in stacks]
        dbasis = [value[0:NB, :] + value[NB : 2 * NB, :] for value in dbasis]
        for value, pair in zip(dbasis, pairs):
            s, reach, fall = radial_parts(pair)
            slope = fall * (-decay * (reach * reach) - (4.0 * s) * reach)
            ds = jnp.sum(value * slope, axis=0, keepdims=True)
            drad_ref[pl.ds(2 * pair, 1), :] = ds[:, 0:EDGE]
            drad_ref[pl.ds(2 * pair + 1, 1), :] = ds[:, EDGE:PE]

    def scatter(step, counts):
        at = pl.ds(pl.multiple_of(step * TS, TS), TS)
        ux, uy, uz = u_ref[0, at, :], u_ref[1, at, :], u_ref[2, at, :]
        twice = 2.0 * drad_ref[at, :]
        dh = [None] + [dharm_ref[m, at, :] for m in range(1, 9)]
        gx = R3 * dh[1] + R15 * (uy * dh[4] + uz * dh[7] + ux * dh[8]) - R5 * (ux * dh[6])
        gy = R3 * dh[2] + R15 * (ux * dh[4] + uz * dh[5] - uy * dh[8]) - R5 * (uy * dh[6])
        gz = R3 * dh[3] + R15 * (uy * dh[5] + ux * dh[7]) + (2.0 * R5) * (uz * dh[6])
        for d, value in enumerate((twice * ux + gx, twice * uy + gy, twice * uz + gz)):
            g = jnp.where(counts, value * INV_CUT, 0.0)
            hi = g.astype(BF16).astype(F32)
            gsep_ref[2 * d] = hi
            gsep_ref[2 * d + 1] = g - hi
        at_high = iota((8, ES), 0) == tiles_of(high_ref, step * TS, TS)
        at_target = hot(iota((128, ES), 0) == tiles_of(target_ref, step * TS, TS))
        at_low = jnp.concatenate([at_ref[step * PER_STEP + q] for q in inner], axis=1)
        row8 = iota((8, ES), 0)
        left, stack = [], jnp.zeros((8, ES), F32)
        for k in range(6):
            value = tiles_of(gsep_ref.at[k], 0, TS)
            left.append(jnp.where(at_high, value, 0.0))
            stack = jnp.where(row8 == k, value, stack)
        acc_ref[...] += dot(jnp.concatenate(left, axis=0).astype(BF16), at_low, 1, 1)
        racc_ref[...] += dot(stack.astype(BF16), at_target, 1, 1)

    def backward(step, carry):
        scatter(lax.rem(step + (STEPS - 2), STEPS), step >= 2)
        to_radius(lax.rem(step + (STEPS - 1), STEPS))
        to_edges(step)
        return carry

    lax.fori_loop(0, STEPS, backward, 0)
    scatter(STEPS - 2, True)
    to_radius(STEPS - 1)
    scatter(STEPS - 1, True)

    for d in range(3):
        grid = acc_ref[16 * d : 16 * d + 8, :] + acc_ref[16 * d + 8 : 16 * d + 16, :]
        for g in range(NG):
            out_grad[g, d : d + 1, :] = grid[g + 1 : g + 2, :]
        mine = racc_ref[2 * d : 2 * d + 1, :] + racc_ref[2 * d + 1 : 2 * d + 2, :]
        force_ref[d] = mine - grid[0:1, :]

    for b in OTHERS:
        pltpu.make_async_remote_copy(
            src_ref=out_grad.at[GROUP[b]],
            dst_ref=in_grad.at[PLACE[26 - b]],
            send_sem=grad_send,
            recv_sem=grad_recv,
            device_id=device(b),
            device_id_type=MESH,
        ).start()
    wait_bytes(in_grad, grad_recv)
    wait_bytes(in_grad, grad_send)

    stacks = []
    for some in GROUPS:
        order = sorted(some, key=lambda b: AT[26 - b])
        came = in_grad[PLACE[order[0]], 0:3, :]
        for b in order[1:]:
            came = jnp.where(lane >= AT[26 - b], in_grad[PLACE[b], 0:3, :], came)
        hi = came.astype(BF16).astype(F32)
        stacks.append(jnp.concatenate([hi, came - hi], axis=0))
    stacks = jnp.concatenate(stacks, axis=1).astype(BF16)
    total = dot(stacks, chosen_ref[...], 1, 1)
    for d in range(3):
        force_ref[d] = force_ref[d] - (total[d : d + 1, :] + total[d + 3 : d + 4, :])


def solution(mesh):
    sizes = tuple(mesh.shape[name] for name in ("gx", "gy", "gz"))
    vmem = pl.BlockSpec(memory_space=pltpu.VMEM)
    hbm = pl.BlockSpec(memory_space=pltpu.HBM)
    pairs = TILES // 2

    def step(
        features,
        positions,
        w_up,
        w_basis,
        w_hidden,
        w_radial,
        w_mix,
        w_read,
        w_out,
        send_lists,
        tile_senders,
        tile_slots,
        tile_bases,
        tile_live,
    ):
        dma = pltpu.SemaphoreType.DMA
        both = pl.pallas_call(
            functools.partial(kernel, sizes),
            out_shape=jax.ShapeDtypeStruct((4, 1, ATOMS), F32),
            in_specs=[hbm] * 14,
            out_specs=vmem,
            scratch_shapes=[
                pltpu.VMEM((ATOMS, C), BF16),
                pltpu.VMEM((3, 1, ATOMS), F32),
                pltpu.VMEM((C, C), BF16),
                pltpu.VMEM((NB, RH), F32),
                pltpu.VMEM((RH, RH), BF16),
                pltpu.VMEM((RH, 3 * C), BF16),
                pltpu.VMEM((3 * C, C), BF16),
                pltpu.VMEM((RO, C), F32),
                pltpu.SMEM((RO,), F32),
                pltpu.VMEM((27, 1, SLOTS), I32),
                pltpu.VMEM((TILES, EDGE), I32),
                pltpu.VMEM((TILES, EDGE), I32),
                pltpu.VMEM((1, TILES), I32),
                pltpu.SMEM((1, 1), I32),
                pltpu.SemaphoreType.DMA((14,)),
                pltpu.VMEM((NG * 128, C), BF16),
                pltpu.VMEM((NG, 4, 128), F32),
                pltpu.VMEM((BLOCKS * 128, C), BF16),
                pltpu.VMEM((26, 4, 128), F32),
                pltpu.VMEM((C, BLOCKS * 128), BF16),
                pltpu.VMEM((BLOCKS, 8, 128), F32),
                pltpu.VMEM((ATOMS, NG * 128), BF16),
                pltpu.VMEM((pairs, 128, PE), BF16),
                pltpu.VMEM((pairs, RH, PE), BF16),
                pltpu.VMEM((pairs, C, PE), BF16),
                pltpu.VMEM((pairs, 3 * C, PE), BF16),
                pltpu.VMEM((pairs, 3 * C, PE), BF16),
                pltpu.VMEM((pairs, 9 * RP, PE), BF16),
                pltpu.VMEM((pairs, RH, PE), F32),
                pltpu.VMEM((pairs, RH, PE), F32),
                pltpu.VMEM((JR, 9 * C), BF16),
                pltpu.VMEM((JR, 9 * C), BF16),
                pltpu.VMEM((3, TILES, EDGE), F32),
                pltpu.VMEM((TILES, EDGE), F32),
                pltpu.VMEM((8, TILES, EDGE), F32),
                pltpu.VMEM((TILES, EDGE), I32),
                pltpu.VMEM((TILES, EDGE), I32),
                pltpu.VMEM((TILES, EDGE), I32),
                pltpu.VMEM((TILES, EDGE), I32),
                pltpu.VMEM((9, TILES, EDGE), F32),
                pltpu.VMEM((TILES, EDGE), F32),
                pltpu.VMEM((6, TS, EDGE), F32),
                pltpu.VMEM((48, 128), F32),
                pltpu.VMEM((8, 128), F32),
                pltpu.VMEM((NG, 4, 128), F32),
                pltpu.VMEM((26, 4, 128), F32),
                pltpu.VMEM((RH, 4 * NB), BF16),
                pltpu.VMEM((RH, RH), BF16),
                pltpu.VMEM((3 * C, RH), BF16),
                pltpu.VMEM((2 * NB, RH), BF16),
                pltpu.VMEM((ATOMS, JR), BF16),
                pltpu.VMEM((JR, ATOMS), BF16),
                dma,
                dma,
                dma,
                dma,
                dma,
                dma,
            ],
            compiler_params=pltpu.CompilerParams(
                collective_id=0,
                has_side_effects=True,
                vmem_limit_bytes=64 * 2**20 - 65536,
            ),
        )(
            features.reshape(ATOMS, C),
            positions.reshape(3, 1, ATOMS),
            w_up,
            w_basis,
            w_hidden,
            w_radial,
            w_mix,
            w_read.T,
            w_out,
            send_lists.reshape(27, 1, SLOTS),
            tile_senders.reshape(TILES, EDGE),
            tile_slots.reshape(TILES, EDGE),
            tile_bases.reshape(1, TILES),
            tile_live.reshape(1, 1),
        )
        return both[0:3].reshape(1, 1, 1, 3, ATOMS), both[3].reshape(1, 1, 1, ATOMS)

    cube = ("gx", "gy", "gz")
    return jax.shard_map(
        step,
        mesh=mesh,
        in_specs=(
            P(*cube, None, None),
            P(*cube, None, None),
            P(),
            P(),
            P(),
            P(),
            P(),
            P(),
            P(),
            P(*cube, None, None, None, None),
            P(*cube, None, None),
            P(*cube, None, None),
            P(*cube, None),
            P(*cube),
        ),
        out_specs=(P(*cube, None, None), P(*cube, None)),
        check_vma=False,
    )
```

```python
import functools

import jax
import jax.numpy as jnp
from jax import lax
from jax.experimental import pallas as pl
from jax.experimental.pallas import tpu as pltpu
from jax.sharding import PartitionSpec as P

MESH = pl.DeviceIdType.MESH
F32 = jnp.float32
BF16 = jnp.bfloat16
I32 = jnp.int32

ATOMS = 128
C = 128
SLOTS = 64
TILES = 64
EDGE = 128
RT = 8
RH = 64
NB = 8
RO = 16
JR = TILES * RT
PE = 2 * EDGE
RP = 2 * RT
PER_STEP = 4
STEPS = TILES // 2 // PER_STEP
BACK = 8
BSTEPS = TILES // 2 // BACK
ES = PE * BACK
NETWORK = 8
TS = 2 * BACK

SIDE = 11.0
INV_CUT = 0.2
R3 = 3.0**0.5
R5 = 5.0**0.5
R15 = 15.0**0.5
DEGREE = (0, 1, 1, 1, 2, 2, 2, 2, 2)
SPANS = ((0, 1), (1, 4), (4, 9))

DIRS = tuple((b // 9 - 1, b // 3 % 3 - 1, b % 3 - 1) for b in range(27))
NONZERO = tuple(sum(v != 0 for v in d) for d in DIRS)
COUNT = tuple(SLOTS * 2 // 2 ** max(k, 1) for k in NONZERO)
OTHERS = tuple(b for b in range(27) if b != 13)


def groups_of():
    groups = []
    for k in (1, 2, 3):
        here = [b for b in OTHERS if NONZERO[b] == k and b < 13]
        per = ATOMS // (SLOTS * 2 // 2**k) // 2
        for first in range(0, len(here), per):
            some = here[first : first + per]
            groups.append(tuple(some) + tuple(26 - b for b in some))
    return tuple(groups)


GROUPS = groups_of()
NG = len(GROUPS)
BLOCKS = NG + 1
PLACE = {b: k for k, b in enumerate(OTHERS)}
GROUP = {b: g for g, some in enumerate(GROUPS) for b in some}
AT = {b: k * COUNT[b] for some in GROUPS for k, b in enumerate(some)}


def dot(a, b, ca, cb, precision=None):
    return lax.dot_general(
        a, b, (((ca,), (cb,)), ((), ())), preferred_element_type=F32, precision=precision
    )


def iota(shape, dim):
    return lax.broadcasted_iota(I32, shape, dim)


def hot(condition):
    return jnp.where(condition, 1.0, 0.0).astype(BF16)


def sigmoid(x):
    return 0.5 + 0.5 * jnp.tanh(0.5 * x)


def split(x):
    hi = x.astype(BF16)
    return hi, (x - hi.astype(F32)).astype(BF16)


def lanes(row, index):
    return jnp.take_along_axis(jnp.broadcast_to(row, index.shape), index, axis=1)


def kernel(
    sizes,
    feat_hbm,
    pos_hbm,
    wup_hbm,
    wbasis_hbm,
    whid_hbm,
    wrad_hbm,
    wmix_hbm,
    wread_hbm,
    wout_hbm,
    lists_hbm,
    send_hbm,
    slot_hbm,
    base_hbm,
    live_hbm,
    force_ref,
    energy_ref,
    feat_ref,
    pos_ref,
    wup_ref,
    wbasis_ref,
    whid_ref,
    wrad_ref,
    wmix_ref,
    wread_ref,
    wout_ref,
    lists_ref,
    send_ref,
    slot_ref,
    base_ref,
    live_ref,
    stage_sem,
    out_rows,
    out_xyz,
    table_b,
    in_xyz,
    table_t,
    table_c,
    chosen_ref,
    at_ref,
    h2_ref,
    rows_ref,
    g_ref,
    a_ref,
    d1_ref,
    d2_ref,
    p_ref,
    s_ref,
    u_ref,
    rad_ref,
    harm_ref,
    slots_ref,
    low_ref,
    high_ref,
    target_ref,
    dharm_ref,
    drad_ref,
    gsep_ref,
    acc_ref,
    racc_ref,
    out_grad,
    in_grad,
    wbt_ref,
    wht_ref,
    wrt_ref,
    wb3_ref,
    placel_ref,
    placer_ref,
    row_send,
    row_recv,
    xyz_send,
    xyz_recv,
    grad_send,
    grad_recv,
):
    here = tuple(lax.axis_index(name) for name in ("gx", "gy", "gz"))

    def device(b):
        return tuple(lax.rem(c + (d + n), n) for c, d, n in zip(here, DIRS[b], sizes))

    staged = {}
    moves = (
        ("lists", lists_hbm, lists_ref),
        ("pos", pos_hbm, pos_ref),
        ("feat", feat_hbm, feat_ref),
        ("wup", wup_hbm, wup_ref),
        ("base", base_hbm, base_ref),
        ("live", live_hbm, live_ref),
        ("slot", slot_hbm, slot_ref),
        ("send", send_hbm, send_ref),
        ("wbasis", wbasis_hbm, wbasis_ref),
        ("whid", whid_hbm, whid_ref),
        ("wrad", wrad_hbm, wrad_ref),
        ("wmix", wmix_hbm, wmix_ref),
        ("wread", wread_hbm, wread_ref),
        ("wout", wout_hbm, wout_ref),
    )
    early = ("lists", "pos", "feat", "wup")
    for k, (name, source, target) in enumerate(moves):
        staged[name] = pltpu.make_async_copy(source, target, stage_sem.at[k])
        if name in early:
            staged[name].start()
    barrier = pltpu.get_barrier_semaphore()
    for b in OTHERS:
        pl.semaphore_signal(barrier, inc=1, device_id=device(b), device_id_type=MESH)
    for name in staged:
        if name not in early:
            staged[name].start()

    staged["lists"].wait()
    staged["pos"].wait()
    own = jnp.concatenate([pos_ref[d] for d in range(3)], axis=0)
    lane = iota((1, 128), 1)
    for g, some in enumerate(GROUPS):
        order = sorted(some, key=lambda b: AT[26 - b])
        named = jnp.concatenate([lists_ref[b][:, 0 : COUNT[b]] for b in order], axis=1)
        chosen_ref[:, 128 * g : 128 * g + 128] = hot(iota((ATOMS, 128), 0) == named)
        for d in range(3):
            shift = jnp.zeros((1, 128), F32)
            for b in some:
                if DIRS[b][d]:
                    inside = (lane >= AT[26 - b]) & (lane < AT[26 - b] + COUNT[b])
                    shift = jnp.where(inside, -SIDE * DIRS[b][d], shift)
            moved = lanes(own[d : d + 1, :], jnp.broadcast_to(named, (8, 128)))[0:1, :]
            out_xyz[g, d : d + 1, :] = moved + shift

    pl.semaphore_wait(barrier, 26)

    for b in OTHERS:
        pltpu.make_async_remote_copy(
            src_ref=out_xyz.at[GROUP[b]],
            dst_ref=in_xyz.at[PLACE[26 - b]],
            send_sem=xyz_send,
            recv_sem=xyz_recv,
            device_id=device(b),
            device_id_type=MESH,
        ).start()
    staged["feat"].wait()
    staged["wup"].wait()
    projected = dot(feat_ref[...], wup_ref[...], 1, 0).astype(BF16)
    table_b[0:ATOMS, :] = projected
    for g in range(NG):
        at = slice(128 * g, 128 * g + 128)
        out_rows[at, :] = dot(chosen_ref[:, at], projected, 0, 0).astype(BF16)
    for b in OTHERS:
        n, g, spot = COUNT[b], GROUP[b], AT[26 - b]
        pltpu.make_async_remote_copy(
            src_ref=out_rows.at[pl.ds(128 * g + spot, n), :],
            dst_ref=table_b.at[pl.ds(128 * (g + 1) + spot, n), :],
            send_sem=row_send,
            recv_sem=row_recv,
            device_id=device(b),
            device_id_type=MESH,
        ).start()

    def wait_bytes(ref, sem):
        pltpu.make_async_copy(ref, ref, sem).wait()

    for name in staged:
        if name not in early:
            staged[name].wait()

    eye = hot(iota((128, 128), 0) == iota((128, 128), 1))
    eye64 = eye[0:64, 0:64]
    wb_hi, wb_lo = split(wbasis_ref[...])
    hi, lo = wb_hi.astype(F32), wb_lo.astype(F32)
    stacked = jnp.concatenate([hi, hi, lo, lo], axis=0).astype(BF16)
    wbt_ref[...] = dot(eye64, stacked, 1, 1).astype(BF16)
    wht_ref[...] = dot(eye64, whid_ref[...], 1, 1).astype(BF16)
    for degree in range(3):
        part = wrad_ref[:, degree * C : degree * C + C]
        wrt_ref[degree * C : degree * C + C, :] = dot(eye, part, 1, 1).astype(BF16)
    wb3_ref[...] = jnp.concatenate([hi, lo], axis=0).astype(BF16)

    base_rows = jnp.broadcast_to(base_ref[...].astype(F32), (128, TILES)).astype(BF16)
    eye_tiles = hot(iota((TILES, TILES), 0) == iota((TILES, TILES), 1))
    base_tiles = dot(eye_tiles, base_rows, 1, 1)
    slots_ref[...] = jnp.where(iota((TILES, EDGE), 0) < live_ref[0, 0], slot_ref[...], RT)
    receiver = base_tiles.astype(I32) + jnp.minimum(slot_ref[...], RT - 1)
    target_ref[...] = receiver

    def place_lanes():
        reach = hot((iota((TILES, JR), 1) >> 3) == iota((TILES, JR), 0))
        expanded = dot(base_rows, reach, 1, 0).astype(I32) + (iota((128, JR), 1) & (RT - 1))
        return hot(expanded == iota((128, JR), 0))

    def place_rows():
        reach = hot((iota((JR, TILES), 0) >> 3) == iota((JR, TILES), 1))
        expanded = dot(reach, base_rows, 1, 1).astype(I32) + (iota((JR, 128), 0) & (RT - 1))
        return hot(expanded == iota((JR, 128), 1))

    placel_ref[...] = place_lanes()
    placer_ref[...] = place_rows()

    block_lane = iota((1, 128), 1)
    moved_by = jnp.zeros((1, 128), I32)
    for b in OTHERS:
        offset = 128 * (GROUP[b] + 1) + AT[b] - (ATOMS + b * SLOTS)
        moved_by = jnp.where(block_lane == b + 2, offset, moved_by)
    for g in range(TILES // 8):
        at = slice(8 * g, 8 * g + 8)
        entry = send_ref[at, :]
        entry = entry + lanes(moved_by, jnp.right_shift(entry, 6))
        low_ref[at, :] = jnp.bitwise_and(entry, 127)
        high_ref[at, :] = jnp.right_shift(entry, 7)

    wait_bytes(in_xyz, xyz_recv)
    wait_bytes(in_xyz, xyz_send)
    for d in range(3):
        table_c[0, d : d + 1, :] = own[d : d + 1, :]
    for g, some in enumerate(GROUPS):
        value = in_xyz[PLACE[some[0]], 0:3, :]
        for b in some[1:]:
            value = jnp.where(lane >= AT[b], in_xyz[PLACE[b], 0:3, :], value)
        table_c[g + 1, 0:3, :] = value

    for g in range(TILES // 8):
        at = slice(8 * g, 8 * g + 8)
        low, high = low_ref[at, :], high_ref[at, :]
        parts = []
        for d in range(3):
            value = lanes(table_c[0, d : d + 1, :], low)
            for k in range(1, BLOCKS):
                value = jnp.where(high == k, lanes(table_c[k, d : d + 1, :], low), value)
            u = (value - lanes(own[d : d + 1, :], receiver[at, :])) * INV_CUT
            u_ref[d, at, :] = u
            parts.append(u)
        ux, uy, uz = parts
        xx, yy, zz = ux * ux, uy * uy, uz * uz
        rad_ref[at, :] = xx + yy + zz
        values = (
            R3 * ux,
            R3 * uy,
            R3 * uz,
            R15 * ux * uy,
            R15 * uy * uz,
            0.5 * R5 * (2.0 * zz - xx - yy),
            R15 * ux * uz,
            0.5 * R15 * (xx - yy),
        )
        for m, value in enumerate(values):
            harm_ref[m, at, :] = value

    decay = (iota((NB, PE), 0).astype(F32) + 1.0) * 0.5
    slot_ids = iota((RP, PE), 0)
    half_shift = jnp.where(iota((1, PE), 1) < EDGE, 0, RT)
    row_ids = iota((128, PE), 0).astype(F32).astype(BF16)
    inner = range(PER_STEP)

    def tiles_of(ref, first, count):
        return jnp.concatenate([ref[pl.ds(first + k, 1), :] for k in range(count)], axis=1)

    def onehot_of(first):
        pair = tiles_of(slots_ref, first, 2)
        pair = jnp.where(pair < RT, pair + half_shift, RP)
        return jnp.where(slot_ids == pair, 1.0, 0.0)

    def radial_parts(pair):
        s = tiles_of(rad_ref, 2 * pair, 2)
        reach = jnp.maximum(1.0 - s * s, 0.0)
        return s, reach, jnp.exp(-decay * s)

    def gather(pair):
        low = tiles_of(low_ref, 2 * pair, 2)
        high = tiles_of(high_ref, 2 * pair, 2)
        at_low = jnp.where(row_ids == low.astype(F32).astype(BF16), jnp.ones((), BF16), jnp.zeros((), BF16))
        at_ref[pair] = at_low
        entries = jnp.concatenate([at_low * hot(high == k) for k in range(BLOCKS)], axis=0)
        rows = dot(table_t[...], entries, 1, 0).astype(BF16)
        rows_ref[pair] = rows
        return rows

    def network(step, carry):
        pairs = [step * NETWORK + q for q in range(NETWORK)]
        basis4 = []
        for pair in pairs:
            s, reach, fall = radial_parts(pair)
            basis = fall * (reach * reach)
            hi = basis.astype(BF16).astype(F32)
            lo = basis - hi
            basis4.append(jnp.concatenate([hi, lo, hi, lo], axis=0).astype(BF16))
        pre1 = [dot(wbt_ref[...], value, 1, 0) for value in basis4]
        act1 = []
        for pair, pre in zip(pairs, pre1):
            sig = sigmoid(pre)
            act = pre * sig
            d1_ref[pair] = sig + act * (1.0 - sig)
            act1.append(act.astype(BF16))
        pre2 = [dot(wht_ref[...], value, 1, 0) for value in act1]
        for pair, pre in zip(pairs, pre2):
            sig = sigmoid(pre)
            act = pre * sig
            d2_ref[pair] = sig + act * (1.0 - sig)
            h2_ref[pair] = act.astype(BF16)
        return carry

    lax.fori_loop(0, TILES // 2 // NETWORK, network, 0)

    wait_bytes(table_b.at[pl.ds(ATOMS, NG * 128), :], row_recv)
    wait_bytes(out_rows, row_send)
    for k in range(BLOCKS):
        block = table_b[128 * k : 128 * k + 128, :]
        table_t[:, 128 * k : 128 * k + 128] = dot(eye, block, 1, 1).astype(BF16)

    def gathered(step, values, radials):
        for q in inner:
            pair = step * PER_STEP + q
            onehot = onehot_of(2 * pair)
            weights = [onehot]
            for m in range(8):
                weights.append(onehot * tiles_of(harm_ref.at[m], 2 * pair, 2))
            weights = jnp.concatenate(weights, axis=0).astype(BF16)
            a_ref[pair] = weights
            rows = values[q]
            place = pl.ds(pair * RP, RP)
            radial = radials[q]
            for degree, (first, last) in enumerate(SPANS):
                across = slice(degree * C, degree * C + C)
                g = radial[across, :] * rows
                g_ref[pair, across, :] = g
                part = dot(weights[first * RP : last * RP, :], g, 1, 1).astype(BF16)
                for m in range(first, last):
                    p_ref[place, m * C : m * C + C] = part[
                        (m - first) * RP : (m - first) * RP + RP, :
                    ]

    def forward(step, carry):
        radials = [dot(wrt_ref[...], h2_ref[step * PER_STEP + q], 1, 0).astype(BF16) for q in inner]
        gathered(step, [gather(step * PER_STEP + q) for q in inner], radials)
        return carry

    lax.fori_loop(0, STEPS, forward, 0)

    sums = dot(placel_ref[...], p_ref[...], 1, 0)
    halves = [0.5 * sums[:, m * C : m * C + C] for m in range(9)]
    inv = [halves[0]]
    for first, last in SPANS[1:]:
        total = halves[first] * halves[first]
        for m in range(first + 1, last):
            total = total + halves[m] * halves[m]
        inv.append(total)
    invariants = jnp.concatenate(inv, axis=1).astype(BF16)
    updated = feat_ref[...].astype(F32) + dot(invariants, wmix_ref[...], 1, 0)
    high = lax.Precision.HIGHEST
    pre = dot(wread_ref[...], updated, 1, 1, high)
    sig = sigmoid(pre)
    act = pre * sig
    row = iota((RO, ATOMS), 0)
    outw = jnp.zeros((RO, ATOMS), F32)
    for r in range(RO):
        outw = jnp.where(row == r, wout_ref[r], outw)
    energy_ref[...] = jnp.sum(outw * act, axis=0, keepdims=True)
    dpre = outw * (sig + act * (1.0 - sig))
    dupd = dot(dpre, wread_ref[...], 0, 0, high)
    dinv = dot(dupd.astype(BF16), wmix_ref[...], 1, 1).astype(BF16).astype(F32)
    grads = []
    for m in range(9):
        part = dinv[:, DEGREE[m] * C : DEGREE[m] * C + C]
        grads.append(0.5 * part if m == 0 else halves[m] * part)
    grads = jnp.concatenate(grads, axis=1).astype(BF16)
    s_ref[...] = dot(placer_ref[...], grads, 1, 0).astype(BF16)

    acc_ref[...] = jnp.zeros_like(acc_ref)
    racc_ref[...] = jnp.zeros_like(racc_ref)

    def cotangents(pair, first, last):
        place = pl.ds(pair * RP, RP)
        return jnp.concatenate(
            [s_ref[place, m * C : m * C + C] for m in range(first, last)], axis=0
        )

    def row_gradients(pair):
        rows = rows_ref[pair]
        parts = []
        for first, last in SPANS:
            cot = cotangents(pair, first, last)
            dg = dot(cot, a_ref[pair, first * RP : last * RP, :], 0, 0)
            parts.append(dg.astype(BF16) * rows)
        return jnp.concatenate(parts, axis=0)

    def harmonic_gradients(pair):
        onehot = onehot_of(2 * pair)
        for degree, (first, last) in enumerate(SPANS):
            if degree:
                across = slice(degree * C, degree * C + C)
                back = dot(cotangents(pair, first, last), g_ref[pair, across, :], 1, 0)
                for m in range(first, last):
                    one = back[(m - first) * RP : (m - first) * RP + RP, :]
                    dh = jnp.sum(one * onehot, axis=0, keepdims=True)
                    dharm_ref[m, pl.ds(2 * pair, 1), :] = dh[:, 0:EDGE]
                    dharm_ref[m, pl.ds(2 * pair + 1, 1), :] = dh[:, EDGE:PE]

    def gradients(step):
        pairs = [step * BACK + q for q in range(BACK)]
        dradial = [row_gradients(pair) for pair in pairs]
        dact2 = [dot(wrad_ref[...], value, 1, 0) for value in dradial]
        dpre2 = [(value * d2_ref[pair]).astype(BF16) for value, pair in zip(dact2, pairs)]
        for pair in pairs[: BACK // 2]:
            harmonic_gradients(pair)
        dact1 = [dot(whid_ref[...], value, 1, 0) for value in dpre2]
        for pair in pairs[BACK // 2 :]:
            harmonic_gradients(pair)
        dpre1 = [(value * d1_ref[pair]).astype(BF16) for value, pair in zip(dact1, pairs)]
        dbasis = [dot(wb3_ref[...], value, 1, 0) for value in dpre1]
        dbasis = [value[0:NB, :] + value[NB : 2 * NB, :] for value in dbasis]
        for value, pair in zip(dbasis, pairs):
            s, reach, fall = radial_parts(pair)
            slope = fall * (-decay * (reach * reach) - (4.0 * s) * reach)
            ds = jnp.sum(value * slope, axis=0, keepdims=True)
            drad_ref[pl.ds(2 * pair, 1), :] = ds[:, 0:EDGE]
            drad_ref[pl.ds(2 * pair + 1, 1), :] = ds[:, EDGE:PE]

    def scatter(step, counts):
        at = pl.ds(pl.multiple_of(step * TS, TS), TS)
        ux, uy, uz = u_ref[0, at, :], u_ref[1, at, :], u_ref[2, at, :]
        twice = 2.0 * drad_ref[at, :]
        dh = [None] + [dharm_ref[m, at, :] for m in range(1, 9)]
        gx = R3 * dh[1] + R15 * (uy * dh[4] + uz * dh[7] + ux * dh[8]) - R5 * (ux * dh[6])
        gy = R3 * dh[2] + R15 * (ux * dh[4] + uz * dh[5] - uy * dh[8]) - R5 * (uy * dh[6])
        gz = R3 * dh[3] + R15 * (uy * dh[5] + ux * dh[7]) + (2.0 * R5) * (uz * dh[6])
        for d, value in enumerate((twice * ux + gx, twice * uy + gy, twice * uz + gz)):
            g = jnp.where(counts, value * INV_CUT, 0.0)
            hi = g.astype(BF16).astype(F32)
            gsep_ref[2 * d] = hi
            gsep_ref[2 * d + 1] = g - hi
        at_high = iota((8, ES), 0) == tiles_of(high_ref, step * TS, TS)
        at_target = jnp.where(iota((128, ES), 0).astype(F32).astype(BF16) == tiles_of(target_ref, step * TS, TS).astype(F32).astype(BF16), jnp.ones((), BF16), jnp.zeros((), BF16))
        at_low = jnp.concatenate([at_ref[step * BACK + q] for q in range(BACK)], axis=1)
        row8 = iota((8, ES), 0)
        left, stack = [], jnp.zeros((8, ES), F32)
        for k in range(6):
            value = tiles_of(gsep_ref.at[k], 0, TS)
            left.append(jnp.where(at_high, value, 0.0))
            stack = jnp.where(row8 == k, value, stack)
        acc_ref[...] += dot(jnp.concatenate(left, axis=0).astype(BF16), at_low, 1, 1)
        racc_ref[...] += dot(stack.astype(BF16), at_target, 1, 1)

    def backward(step, carry):
        scatter(lax.rem(step + (BSTEPS - 1), BSTEPS), step >= 1)
        gradients(step)
        return carry

    lax.fori_loop(0, BSTEPS, backward, 0)
    scatter(BSTEPS - 1, True)

    for d in range(3):
        grid = acc_ref[16 * d : 16 * d + 8, :] + acc_ref[16 * d + 8 : 16 * d + 16, :]
        for g in range(NG):
            out_grad[g, d : d + 1, :] = grid[g + 1 : g + 2, :]
        mine = racc_ref[2 * d : 2 * d + 1, :] + racc_ref[2 * d + 1 : 2 * d + 2, :]
        force_ref[d] = mine - grid[0:1, :]

    for b in OTHERS:
        pltpu.make_async_remote_copy(
            src_ref=out_grad.at[GROUP[b]],
            dst_ref=in_grad.at[PLACE[26 - b]],
            send_sem=grad_send,
            recv_sem=grad_recv,
            device_id=device(b),
            device_id_type=MESH,
        ).start()
    wait_bytes(in_grad, grad_recv)
    wait_bytes(in_grad, grad_send)

    stacks = []
    for some in GROUPS:
        order = sorted(some, key=lambda b: AT[26 - b])
        came = in_grad[PLACE[order[0]], 0:3, :]
        for b in order[1:]:
            came = jnp.where(lane >= AT[26 - b], in_grad[PLACE[b], 0:3, :], came)
        hi = came.astype(BF16).astype(F32)
        stacks.append(jnp.concatenate([hi, came - hi], axis=0))
    stacks = jnp.concatenate(stacks, axis=1).astype(BF16)
    total = dot(stacks, chosen_ref[...], 1, 1)
    for d in range(3):
        force_ref[d] = force_ref[d] - (total[d : d + 1, :] + total[d + 3 : d + 4, :])


def solution(mesh):
    sizes = tuple(mesh.shape[name] for name in ("gx", "gy", "gz"))
    vmem = pl.BlockSpec(memory_space=pltpu.VMEM)
    hbm = pl.BlockSpec(memory_space=pltpu.HBM)
    pairs = TILES // 2

    def step(
        features,
        positions,
        w_up,
        w_basis,
        w_hidden,
        w_radial,
        w_mix,
        w_read,
        w_out,
        send_lists,
        tile_senders,
        tile_slots,
        tile_bases,
        tile_live,
    ):
        dma = pltpu.SemaphoreType.DMA
        force, energy = pl.pallas_call(
            functools.partial(kernel, sizes),
            out_shape=(
                jax.ShapeDtypeStruct((3, 1, ATOMS), F32),
                jax.ShapeDtypeStruct((1, ATOMS), F32),
            ),
            in_specs=[hbm] * 14,
            out_specs=(vmem, vmem),
            scratch_shapes=[
                pltpu.VMEM((ATOMS, C), BF16),
                pltpu.VMEM((3, 1, ATOMS), F32),
                pltpu.VMEM((C, C), BF16),
                pltpu.VMEM((NB, RH), F32),
                pltpu.VMEM((RH, RH), BF16),
                pltpu.VMEM((RH, 3 * C), BF16),
                pltpu.VMEM((3 * C, C), BF16),
                pltpu.VMEM((RO, C), F32),
                pltpu.SMEM((RO,), F32),
                pltpu.VMEM((27, 1, SLOTS), I32),
                pltpu.VMEM((TILES, EDGE), I32),
                pltpu.VMEM((TILES, EDGE), I32),
                pltpu.VMEM((1, TILES), I32),
                pltpu.SMEM((1, 1), I32),
                pltpu.SemaphoreType.DMA((14,)),
                pltpu.VMEM((NG * 128, C), BF16),
                pltpu.VMEM((NG, 4, 128), F32),
                pltpu.VMEM((BLOCKS * 128, C), BF16),
                pltpu.VMEM((26, 4, 128), F32),
                pltpu.VMEM((C, BLOCKS * 128), BF16),
                pltpu.VMEM((BLOCKS, 8, 128), F32),
                pltpu.VMEM((ATOMS, NG * 128), BF16),
                pltpu.VMEM((pairs, 128, PE), BF16),
                pltpu.VMEM((pairs, RH, PE), BF16),
                pltpu.VMEM((pairs, C, PE), BF16),
                pltpu.VMEM((pairs, 3 * C, PE), BF16),
                pltpu.VMEM((pairs, 9 * RP, PE), BF16),
                pltpu.VMEM((pairs, RH, PE), F32),
                pltpu.VMEM((pairs, RH, PE), F32),
                pltpu.VMEM((JR, 9 * C), BF16),
                pltpu.VMEM((JR, 9 * C), BF16),
                pltpu.VMEM((3, TILES, EDGE), F32),
                pltpu.VMEM((TILES, EDGE), F32),
                pltpu.VMEM((8, TILES, EDGE), F32),
                pltpu.VMEM((TILES, EDGE), I32),
                pltpu.VMEM((TILES, EDGE), I32),
                pltpu.VMEM((TILES, EDGE), I32),
                pltpu.VMEM((TILES, EDGE), I32),
                pltpu.VMEM((9, TILES, EDGE), F32),
                pltpu.VMEM((TILES, EDGE), F32),
                pltpu.VMEM((6, TS, EDGE), F32),
                pltpu.VMEM((48, 128), F32),
                pltpu.VMEM((8, 128), F32),
                pltpu.VMEM((NG, 4, 128), F32),
                pltpu.VMEM((26, 4, 128), F32),
                pltpu.VMEM((RH, 4 * NB), BF16),
                pltpu.VMEM((RH, RH), BF16),
                pltpu.VMEM((3 * C, RH), BF16),
                pltpu.VMEM((2 * NB, RH), BF16),
                pltpu.VMEM((ATOMS, JR), BF16),
                pltpu.VMEM((JR, ATOMS), BF16),
                dma,
                dma,
                dma,
                dma,
                dma,
                dma,
            ],
            compiler_params=pltpu.CompilerParams(
                collective_id=0,
                has_side_effects=True,
                vmem_limit_bytes=64 * 2**20 - 65536,
            ),
        )(
            features.reshape(ATOMS, C),
            positions.reshape(3, 1, ATOMS),
            w_up,
            w_basis,
            w_hidden,
            w_radial,
            w_mix,
            w_read.T,
            w_out,
            send_lists.reshape(27, 1, SLOTS),
            tile_senders.reshape(TILES, EDGE),
            tile_slots.reshape(TILES, EDGE),
            tile_bases.reshape(1, TILES),
            tile_live.reshape(1, 1),
        )
        return force.reshape(1, 1, 1, 3, ATOMS), energy.reshape(1, 1, 1, ATOMS)

    cube = ("gx", "gy", "gz")
    return jax.shard_map(
        step,
        mesh=mesh,
        in_specs=(
            P(*cube, None, None),
            P(*cube, None, None),
            P(),
            P(),
            P(),
            P(),
            P(),
            P(),
            P(),
            P(*cube, None, None, None, None),
            P(*cube, None, None),
            P(*cube, None, None),
            P(*cube, None),
            P(*cube),
        ),
        out_specs=(P(*cube, None, None), P(*cube, None)),
        check_vma=False,
    )
```
